128 devices in a mesh: slab: 16 (over z, y), pair: 8 (over x, core).
Axes of the slice: x: 4, y: 4, z: 4, core: 2. Of those that a mesh axis runs over, the one named last changes fastest.
Arguments:
- amplitudes: bfloat16 [512, 8, 128, 192], P(('pair', 'slab')), may hold values from -6 to 6
- integrals: bfloat16 [128, 8, 192, 6144], P('slab', None, None, 'pair'), may hold values from -0.046875 to 0.046875
- vir_counts: int32 [8], replicated, may hold values from 1 to 192, 1200 in all
- c_orbitals: int32 [128], replicated, may hold values from 0 to 1199
- a_orbitals: int32 [32], replicated, may hold values from 0 to 1199
Outputs:
- residual: float32 [512, 8, 6144], P(('pair', 'slab'))
The draws below stay inside these ranges and needn't reach their ends.
Inputs may be any that keep to these rules, and one draw needn't show every extreme that they name: Virtual orbitals are numbered irrep by irrep, vir_counts[g] of irrep g; the counts sum to 1200 and the largest is 192.
All inputs are finite; a program needn't handle non-finite values.
Results may differ from the reference program's by a relative error of at most 0.0003.
Values may be sent and summed in bfloat16 or wider, within the bound.
No kernel may reach another device: no remote copies, remote signals or barrier semaphores. Data moves between devices by JAX's collectives and lax.ppermute only.
A program may use at most 192 MiB of HBM per device.

```python
import math
import jax
import jax.numpy as jnp
import numpy as np
from jax import lax

NVIR = 1200
IRREPS = 8
DMAX = 192
C_DEV = 8
C_TOT = 128
A_WIN = 32
PAIRS_IRR = 512


def with_ends(entries, own_key, low, largest):
    index_at = [jax.random.randint(jax.random.fold_in(own_key, axis), (), 0, length) for axis, length in enumerate(entries.shape)]
    main_axis = entries.shape.index(max(entries.shape))
    beside = index_at[:main_axis] + [(index_at[main_axis] + 1) % entries.shape[main_axis]] + index_at[main_axis + 1:]
    return entries.at[tuple(index_at)].set(low).at[tuple(beside)].set(largest)


def level_of(own_key, shape, pieces, smallest, high):
    gain, own = 1.0, jax.random.fold_in(own_key, 6)
    for axis_at, shards_of in pieces:
        heights = jnp.exp(jax.random.uniform(jax.random.fold_in(own, axis_at), (shards_of,), jnp.float32, smallest / len(pieces), high / len(pieces)))
        gain = gain * jnp.repeat(heights, shape[axis_at] // shards_of).reshape([-1 if axis == axis_at else 1 for axis in range(len(shape))])
    return gain


def length_profile(amount, total, most, slope):
    weights = [(1 << 20) // math.isqrt(grade ** slope) + 1 for grade in range(2, amount + 1)]
    surplus, counts = total - most - (amount - 1), [1] * (amount - 1)
    while surplus > 0:
        candidates = [i for i in range(amount - 1) if counts[i] < most]
        mass, left = sum([weights[i] for i in candidates]), surplus
        for i in candidates:
            addition = min(most - counts[i], max(1, left * weights[i] // mass), surplus)
            counts[i] = counts[i] + addition
            surplus = surplus - addition
    return np.array([most] + counts)


def uneven(rng, amount, total, limit, slope):
    if amount == 2:
        one = jax.random.randint(rng, (), max(1, total - limit), min(limit, total - 1) + 1)
        return jnp.stack([one, total - one])
    tallies = jnp.asarray(length_profile(amount, total, limit, slope), jnp.int32)
    pairs = (amount - 1) // 2
    source_of, taker = tallies[1:1 + 2 * pairs:2], tallies[2:2 + 2 * pairs:2]
    margin = jnp.minimum(source_of - 1, limit - taker)
    passed = jax.random.randint(jax.random.fold_in(rng, 1), (pairs,), 0, 1 << 20) % (margin + 1)
    tallies = tallies.at[1:1 + 2 * pairs:2].set(source_of - passed).at[2:2 + 2 * pairs:2].set(taker + passed)
    return tallies[jax.random.permutation(jax.random.fold_in(rng, 2), amount)]


def normal_values(key, shape, deviation, bound, cuts=(), kind=jnp.bfloat16):
    array = jax.random.normal(key, shape, jnp.float32) * deviation
    if len(cuts) > 0:
        array = level_of(key, shape, cuts, -0.22, 0.18) * array
    return jnp.clip(array, min=-bound, max=bound).astype(kind)


def setup_inputs(seed: int = 0) -> dict:
    seeds = jax.random.split(jax.random.key(seed), 6)
    return {
        "amplitudes": normal_values(seeds[0], (PAIRS_IRR, IRREPS, C_TOT, DMAX), 1.0, 6.0, ((0, 128),)),
        "integrals": normal_values(seeds[1], (C_TOT, IRREPS, DMAX, A_WIN * DMAX), (C_TOT * NVIR // IRREPS) ** -0.5, 0.046875, ((0, 16), (3, 8))),
        "vir_counts": uneven(seeds[2], IRREPS, NVIR, DMAX, 1).astype(jnp.int32),
        "c_orbitals": with_ends(jax.random.randint(seeds[3], (C_TOT,), 0, NVIR), jax.random.fold_in(seeds[3], 1), 0, NVIR - 1).astype(jnp.int32),
        "a_orbitals": with_ends(jax.random.randint(seeds[4], (A_WIN,), 0, NVIR), jax.random.fold_in(seeds[4], 1), 0, NVIR - 1).astype(jnp.int32),
    }


def irrep_of(orbitals, vir_counts):
    ends = jnp.cumsum(vir_counts, dtype=jnp.int32)
    return jnp.sum((orbitals[:, None] >= ends[None, :]).astype(jnp.int32), axis=1, dtype=jnp.int32)


def reference(amplitudes, integrals, vir_counts, c_orbitals, a_orbitals):
    irreps = vir_counts.shape[0]
    dmax = amplitudes.shape[3]
    pairs = amplitudes.shape[0]
    c_tot = amplitudes.shape[2]
    columns = integrals.shape[3]
    labels = jnp.arange(irreps, dtype=jnp.int32)
    slots = jnp.arange(dmax, dtype=jnp.int32)
    c_irrep = irrep_of(c_orbitals, vir_counts)
    a_irrep = irrep_of(a_orbitals, vir_counts)
    c_blocks = jnp.bitwise_xor(labels[:, None], c_irrep[None, :])
    c_limit = vir_counts[c_blocks]
    keep = slots[None, None, :] < c_limit[:, :, None]
    kept = jnp.where(keep[None], amplitudes, jnp.zeros((), amplitudes.dtype))
    nblocks = c_tot // C_DEV
    kept_blocks = kept.reshape(pairs, irreps, nblocks, C_DEV * dmax)
    local = jnp.arange(C_DEV, dtype=jnp.int32)

    def step(total, index):
        start = index * C_DEV
        slab_part = lax.dynamic_slice_in_dim(integrals, start, C_DEV, 0)
        blocks = lax.dynamic_slice_in_dim(c_blocks, start, C_DEV, 1)
        weights = slab_part[local[None, :], blocks].reshape(irreps, C_DEV * dmax, columns).astype(jnp.float32)
        left = lax.dynamic_index_in_dim(kept_blocks, index, 2, keepdims=False).astype(jnp.float32)
        return total + jnp.einsum("mpk,pkn->mpn", left, weights), None

    total, _ = lax.scan(step, jnp.zeros((pairs, irreps, columns), jnp.float32), jnp.arange(nblocks, dtype=jnp.int32))
    a_blocks = jnp.bitwise_xor(labels[:, None], a_irrep[None, :])
    allow = slots[None, None, :] < vir_counts[a_blocks][:, :, None]
    shaped = total.reshape(pairs, irreps, a_orbitals.shape[0], dmax)
    result = jnp.where(allow[None], shaped, jnp.zeros((), shaped.dtype))
    return result.reshape(pairs, irreps, columns)
```

```python
import functools

import jax
import jax.numpy as jnp
from jax import lax
from jax.experimental import pallas as pl
from jax.experimental.pallas import tpu as pltpu
from jax.sharding import PartitionSpec as P

CHUNKS = 2
TOP = 32766.0
FINE = 256.0
AXES = ("slab", "pair")


def irrep_of(orbitals, vir_counts):
    ends = jnp.cumsum(vir_counts, dtype=jnp.int32)
    return jnp.sum((orbitals[:, None] >= ends[None, :]).astype(jnp.int32), axis=1, dtype=jnp.int32)


def limits(labels_of, vir_counts):
    labels = jnp.arange(vir_counts.shape[0], dtype=jnp.int32)
    blocks = jnp.bitwise_xor(labels[:, None], labels_of[None, :])
    picked = jnp.where(blocks[:, :, None] == labels[None, None, :], vir_counts[None, None, :], 0)
    return jnp.sum(picked, axis=2, dtype=jnp.int32)


def moves(target):
    def place(z, y, x, core):
        return ((z % 4) * 4 + y % 4) * 8 + (x % 4) * 2 + core

    return [
        (place(z, y, x, core), place(*target(z, y, x, core)))
        for z in range(4) for y in range(4) for x in range(4) for core in range(2)
    ]


X_UP = moves(lambda z, y, x, core: (z, y, x + 1, core))
X_DOWN = moves(lambda z, y, x, core: (z, y, x - 1, core))
SWAP = moves(lambda z, y, x, core: (z, y, x, 1 - core))


def first(k):
    return moves(lambda z, y, x, core: (z, y + k, x, core) if core == 0 else (z + k, y, x, core))


def second(k):
    return moves(lambda z, y, x, core: (z + k, y, x, core) if core == 0 else (z, y + k, x, core))


def send(value, pairs):
    return lax.ppermute(value, AXES, pairs)


def matmul_kernel(m, irrep_ref, *refs):
    arrays, v_ref, own_ref = refs[:10], refs[10], refs[11]
    coded, (lhs, mix, codes, slots, sems) = refs[12:15], refs[15:]
    p = pl.program_id(0)
    rows = 16 * m
    c_dev, depth = slots.shape[1] // 192, 192

    def fetch(step, slot):
        return [
            pltpu.make_async_copy(
                v_ref.at[c, jnp.bitwise_xor(step, irrep_ref[c])],
                slots.at[slot, pl.ds(c * depth, depth)],
                sems.at[slot, c],
            )
            for c in range(c_dev)
        ]

    @pl.when(p == 0)
    def _():
        for copy in fetch(0, 0):
            copy.start()
        size = 128 * m
        r = lax.broadcasted_iota(jnp.int32, (size, size), 0)
        col = lax.broadcasted_iota(jnp.int32, (size, size), 1)
        pair = lax.rem(r, m)
        x_rel = lax.rem(lax.div(r, m), 4)
        other = lax.rem(lax.div(r, 4 * m), 2)
        d2 = lax.rem(lax.div(r, 8 * m), 4)
        d1 = lax.div(r, 32 * m)
        major = jnp.where(other == 0, d1, d2)
        minor = jnp.where(other == 0, d2, d1)
        source = other * (64 * m) + x_rel * (16 * m) + major * (4 * m) + minor * m + pair
        mix[...] = (source == col).astype(jnp.float32).astype(jnp.bfloat16)
        codes[...] = jnp.zeros_like(codes)

    @pl.when(p < 7)
    def _():
        for copy in fetch(p + 1, lax.rem(p + 1, 2)):
            copy.start()

    a0, a1, a3, ha, hb, o0, o1, o3, oa, ob = arrays
    low = p < 4
    for base, (r0, r1, r3, half_a, half_b) in ((0, (a0, a1, a3, ha, hb)), (4, (o0, o1, o3, oa, ob))):
        for at, ref in ((0, r0), (1, r1), (3, r3)):
            lhs[pl.ds((base + at) * rows, rows), :] = ref[...]

        @pl.when(low)
        def _():
            lhs[pl.ds((base + 2) * rows, rows), :] = half_a[...]

        @pl.when(jnp.logical_not(low))
        def _():
            lhs[pl.ds((base + 2) * rows, rows), :] = half_b[...]

    mixed = jnp.dot(mix[...], lhs[...], preferred_element_type=jnp.float32).astype(jnp.bfloat16)
    slot = lax.rem(p, 2)
    for copy in fetch(p, slot):
        copy.wait()
    product = jnp.dot(mixed, slots[slot], preferred_element_type=jnp.float32)
    piece = 32 * m
    columns = product.shape[1]
    at = pl.ds(pl.multiple_of(p * columns, 128), columns)
    own_ref[:, at] = product[:piece]
    lane = lax.broadcasted_iota(jnp.int32, (piece, 128), 1)
    for k in range(1, 4):
        part = product[k * piece:(k + 1) * piece]
        peak = jnp.maximum(jnp.max(jnp.abs(part), axis=1, keepdims=True), 2.0**-100)
        code = jnp.ceil(jnp.log2(peak) * FINE)
        coded[k - 1][:, at] = jnp.round(part * (jnp.exp2(code * (-1.0 / FINE)) * TOP)).astype(jnp.int16)
        codes[k - 1] = jnp.where(lane == p, code, codes[k - 1])

    @pl.when(p == 7)
    def _():
        for k in range(3):
            coded[k][:, pl.ds(8 * columns, 128)] = codes[k].astype(jnp.int16)


def matmul(arrays, integrals, irreps, m):
    rows, depth = 16 * m, arrays[0].shape[1]
    columns = integrals.shape[3]
    whole = pl.BlockSpec((rows, depth), lambda p, irr: (p, 0))
    low = pl.BlockSpec((rows, depth), lambda p, irr: (jnp.minimum(p, 3), 0))
    high = pl.BlockSpec((rows, depth), lambda p, irr: (jnp.maximum(p - 4, 0), 0))
    five = [whole, whole, whole, low, high]
    piece = 32 * m
    shapes = [jax.ShapeDtypeStruct((piece, 8 * columns), jnp.float32)]
    shapes += [jax.ShapeDtypeStruct((piece, 8 * columns + 128), jnp.int16)] * 3
    return pl.pallas_call(
        functools.partial(matmul_kernel, m),
        grid_spec=pltpu.PrefetchScalarGridSpec(
            num_scalar_prefetch=1,
            grid=(8,),
            in_specs=five + five + [pl.BlockSpec(memory_space=pl.ANY)],
            out_specs=[pl.BlockSpec(s.shape, lambda p, irr: (0, 0)) for s in shapes],
            scratch_shapes=[
                pltpu.VMEM((8 * rows, depth), jnp.bfloat16),
                pltpu.VMEM((8 * rows, 8 * rows), jnp.bfloat16),
                pltpu.VMEM((3, piece, 128), jnp.float32),
                pltpu.VMEM((2, depth, columns), jnp.bfloat16),
                pltpu.SemaphoreType.DMA((2, 8)),
            ],
        ),
        out_shape=shapes,
        compiler_params=pltpu.CompilerParams(vmem_limit_bytes=48 * 2**20),
        cost_estimate=pl.CostEstimate(
            flops=2 * 8 * 8 * rows * depth * columns, bytes_accessed=integrals.size * 2, transcendentals=0
        ),
    )(irreps, *arrays, integrals)


def sum_kernel(own, q1, q2, q3, s1, s2, s3, *outs):
    p = pl.program_id(0)
    total = own[...]
    lane = lax.broadcasted_iota(jnp.int32, s1.shape, 1)
    for q, s in ((q1, s1), (q2, s2), (q3, s3)):
        code = jnp.sum(jnp.where(lane == p, s[...].astype(jnp.float32), 0.0), axis=1, keepdims=True)
        total += q[...].astype(jnp.float32) * (jnp.exp2(code * (1.0 / FINE)) * (1.0 / TOP))
    each = total.shape[0] // 4
    for k in range(4):
        outs[k][...] = total[k * each:(k + 1) * each]


def sum_coded(own, parts):
    piece, width = own.shape
    columns = width // 8
    block = pl.BlockSpec((piece, columns), lambda p: (0, p))
    scale = pl.BlockSpec((piece, 128), lambda p: (0, width // 128))
    out = pl.BlockSpec((piece // 4, columns), lambda p: (0, p))
    return pl.pallas_call(
        sum_kernel,
        grid=(8,),
        in_specs=[block] * 4 + [scale] * 3,
        out_specs=[out] * 4,
        out_shape=[jax.ShapeDtypeStruct((piece // 4, width), jnp.float32)] * 4,
        cost_estimate=pl.CostEstimate(flops=8 * own.size, bytes_accessed=14 * own.size, transcendentals=0),
    )(own, *parts, *parts)


def shards(amplitudes, integrals, vir_counts, c_orbitals, a_orbitals):
    irreps = vir_counts.shape[0]
    dmax = amplitudes.shape[3]
    slots = jnp.arange(dmax, dtype=jnp.int32)
    c_irrep = irrep_of(c_orbitals, vir_counts)
    a_irrep = irrep_of(a_orbitals, vir_counts)
    keep = slots[None, None, :] < limits(c_irrep, vir_counts)[:, :, None]
    kept = jnp.where(keep[None], amplitudes, jnp.zeros((), amplitudes.dtype))
    n_slab = lax.axis_size("slab")
    c_dev = amplitudes.shape[2] // n_slab
    slab, pair = lax.axis_index("slab"), lax.axis_index("pair")
    z, y, x, core = slab // 4, slab % 4, pair // 2, pair % 2
    own_irrep = lax.dynamic_slice_in_dim(c_irrep, slab * c_dev, c_dev, 0)
    rows = amplitudes.shape[0]
    m = rows // CHUNKS
    depth = c_dev * dmax
    columns = integrals.shape[3]
    a_win = a_orbitals.shape[0]

    size = n_slab * m * irreps
    r = jnp.arange(size, dtype=jnp.int32)
    minor, d2, d1, label = r % m, r // m % 4, r // (4 * m) % 4, r // (16 * m)
    dy = jnp.where(core == 0, d1, d2)
    dz = jnp.where(core == 0, d2, d1)
    source = (((z + dz) % 4 * 4 + (y + dy) % 4) * m + minor) * irreps + label
    chooser = (source[:, None] == r[None, :]).astype(jnp.bfloat16)

    j = jnp.arange(8, dtype=jnp.int32)
    from_rel = ((j % 2) ^ core) * 4 + (j // 2 - x) % 4

    by_slab = kept.reshape(rows, irreps, n_slab, depth).transpose(2, 0, 1, 3)
    results = []
    for chunk in range(CHUNKS):
        piece = by_slab[:, chunk * m:(chunk + 1) * m]
        got = lax.all_to_all(piece, "slab", split_axis=0, concat_axis=0, tiled=True)
        a0 = jnp.dot(chooser, got.reshape(size, depth), preferred_element_type=jnp.float32).astype(jnp.bfloat16)
        a1, a3 = send(a0, X_DOWN), send(a0, X_UP)
        ha, hb = send(a1[:size // 2], X_DOWN), send(a3[size // 2:], X_UP)
        mine = [a0, a1, a3, ha, hb]
        theirs = [send(v, SWAP) for v in mine]
        own, q1, q2, q3 = matmul(mine + theirs, integrals, own_irrep, m)
        parts = [send(q, first(k)) for k, q in ((1, q1), (2, q2), (3, q3))]
        t0, t1, t2, t3 = sum_coded(own, parts)
        total = t0 + send(t1, second(1)) + send(t2, second(2)) + send(t3, second(3))
        blocks = total.reshape(8, m, irreps * columns)[from_rel]
        back = lax.all_to_all(blocks, "pair", split_axis=0, concat_axis=0, tiled=True)
        results.append(back.reshape(8, m, irreps, columns).transpose(1, 2, 0, 3).reshape(m, irreps, 8 * columns))
    full = jnp.concatenate(results, axis=0)
    allow = slots[None, None, :] < limits(a_irrep, vir_counts)[:, :, None]
    shaped = full.reshape(rows, irreps, a_win, dmax)
    result = jnp.where(allow[None], shaped, jnp.zeros((), jnp.float32))
    return result.reshape(rows, irreps, a_win * dmax)


def solution(mesh):
    in_specs = (P(("pair", "slab"), None, None, None), P("slab", None, None, "pair"), P(), P(), P())
    out_specs = P(("pair", "slab"), None, None)
    return jax.shard_map(shards, mesh=mesh, in_specs=in_specs, out_specs=out_specs, check_vma=False)
```

```python
import functools

import jax
import jax.numpy as jnp
from jax import lax
from jax.experimental import pallas as pl
from jax.experimental.pallas import tpu as pltpu
from jax.sharding import PartitionSpec as P

SPLIT = (4, 4)
TOP = 32766.0
FINE = 256.0
AXES = ("slab", "pair")
MIB = 2**20
LIMIT = 58
HBM = pl.BlockSpec(memory_space=pl.ANY)
VMEM = pl.BlockSpec(memory_space=pltpu.VMEM)
SMEM = pl.BlockSpec(memory_space=pltpu.SMEM)


def place(z, y, x, core):
    return ((z % 4) * 4 + y % 4) * 8 + (x % 4) * 2 + core


def moves(target):
    return [
        (place(z, y, x, core), place(*target(z, y, x, core)))
        for z in range(4) for y in range(4) for x in range(4) for core in range(2)
    ]


X_UP = moves(lambda z, y, x, core: (z, y, x + 1, core))
X_DOWN = moves(lambda z, y, x, core: (z, y, x - 1, core))
SWAP = moves(lambda z, y, x, core: (z, y, x, 1 - core))
GROUPS = [[place(z, y, x, 0) for x in range(4) for z in range(4)] for y in range(4)]
GROUPS += [[place(z, y, x, 1) for x in range(4) for y in range(4)] for z in range(4)]


def first(k):
    return moves(lambda z, y, x, core: (z, y + k, x, core) if core == 0 else (z + k, y, x, core))


def send(value, pairs):
    return lax.ppermute(value, AXES, pairs)


def cost(flops, size):
    return pl.CostEstimate(flops=flops, bytes_accessed=size, transcendentals=0)


def params(size):
    return pltpu.CompilerParams(vmem_limit_bytes=size * MIB)


def one_hot(rows, source):
    r = lax.broadcasted_iota(jnp.int32, (rows, rows), 0)
    col = lax.broadcasted_iota(jnp.int32, (rows, rows), 1)
    return (source(r) == col).astype(jnp.float32).astype(jnp.bfloat16)


def pick(matrix, value):
    return jnp.dot(matrix, value, preferred_element_type=jnp.float32)


def code_of(part):
    peak = jnp.maximum(jnp.max(jnp.abs(part), axis=1, keepdims=True), 2.0**-100)
    code = jnp.ceil(jnp.log2(peak) * FINE)
    return code, jnp.round(part * (jnp.exp2(code * (-1.0 / FINE)) * TOP))


def ends_of(counts):
    ends, total = [], 0
    for g in range(8):
        total = total + counts[g]
        ends.append(total)
    return ends


def arrange_kernel(start, counts, c_ref, t_ref, out, sorted_ref):
    pairs, count, dmax, c_tot = t_ref.shape
    n_slab = c_tot // 8
    rows = pairs * count
    ends = ends_of(counts)
    orbital = c_ref[...]
    irrep = sum((orbital >= ends[g]).astype(jnp.int32) for g in range(8))
    slot = lax.broadcasted_iota(jnp.int32, (dmax, c_tot), 0)
    by_c = one_hot(c_tot, lambda r: lax.rem(r, n_slab) * 8 + lax.div(r, n_slab))
    for p in range(count):
        block = jnp.bitwise_xor(irrep, start + p)
        limit = sum(jnp.where(block == g, counts[g], 0) for g in range(8))
        keep = slot < limit
        for pair in range(pairs):
            kept = jnp.where(keep, t_ref[pair, p].astype(jnp.float32), 0.0).astype(jnp.bfloat16)
            split = lax.dot_general(by_c, kept, (((1,), (1,)), ((), ())), preferred_element_type=jnp.float32)
            split = split.astype(jnp.bfloat16)
            q = pair * count + p
            for c in range(8):
                sorted_ref[c, q * n_slab:(q + 1) * n_slab] = split[c * n_slab:(c + 1) * n_slab]
    by_slab = one_hot(n_slab * rows, lambda r: lax.rem(r, rows) * n_slab + lax.div(r, rows))
    for i in range(4):
        both = [pick(by_slab, sorted_ref[2 * i + h]) for h in range(2)]
        out[:, i * 2 * dmax:(i + 1) * 2 * dmax] = jnp.concatenate(both, axis=1).astype(jnp.bfloat16)


def arrange(amplitudes, vir_counts, c_orbitals, start, count):
    rows, _, dmax, c_tot = amplitudes.shape
    size = c_tot // 8 * rows * count
    return pl.pallas_call(
        functools.partial(arrange_kernel, start),
        grid=(1,),
        in_specs=[
            SMEM,
            pl.BlockSpec((1, c_tot), lambda i: (0, 0)),
            pl.BlockSpec((rows, count, dmax, c_tot), lambda i: (0, start // count, 0, 0)),
        ],
        out_specs=pl.BlockSpec((size, 8 * dmax), lambda i: (0, 0)),
        out_shape=jax.ShapeDtypeStruct((size, 8 * dmax), jnp.bfloat16),
        scratch_shapes=[pltpu.VMEM((8, size, dmax), jnp.bfloat16)],
        compiler_params=params(LIMIT),
        cost_estimate=cost(2 * 10**9, 4 * 10**6),
    )(vir_counts, c_orbitals.reshape(1, c_tot), amplitudes)


def matmul_kernel(m, start, counts, c_orbitals, *refs):
    lows, highs, (v_own, v_other) = refs[:4], refs[4:8], refs[8:10]
    outs = refs[10:14]
    lhs, slots, even, odd, own, coded, codes, sems, v_sems, o_sems = refs[14:]
    number, _, rows, depth = lhs.shape
    c_dev, _, dmax, half = v_own.shape
    width = 2 * half
    split = lows[0].shape[0]
    slab, pair = lax.axis_index("slab"), lax.axis_index("pair")
    x, core = lax.div(pair, 2), lax.rem(pair, 2)
    me = jnp.where(core == 0, lax.rem(slab, 4), lax.div(slab, 4))
    ends = ends_of(counts)
    irreps = []
    for c in range(c_dev):
        orbital = c_orbitals[slab * c_dev + c]
        irreps.append(sum((orbital >= ends[g]).astype(jnp.int32) for g in range(8)))

    def fetch(p):
        return [
            pltpu.make_async_copy(
                ref.at[c, jnp.bitwise_xor(irreps[c], start + p)],
                slots.at[p % 3, side, pl.ds(c * dmax, dmax)],
                v_sems.at[p % 3, side, c],
            )
            for side, ref in ((0, v_own), (1, v_other)) for c in range(c_dev)
        ]

    def arrivals(refs, first_p, at):
        return [
            pltpu.make_async_copy(ref, lhs.at[pl.ds(first_p, ref.shape[0]), lax.rem(x + r, 4)], sems.at[at + r])
            for r, ref in enumerate(refs)
        ]

    low, high = arrivals(lows, 0, 0), arrivals(highs, split, 4)
    for copy in low + fetch(0) + high + fetch(1):
        copy.start()
    codes[...] = jnp.zeros_like(codes)
    lane = lax.broadcasted_iota(jnp.int32, (rows, 128), 1)
    started = []

    def finish(p, ref):
        at = slice(p * width, (p + 1) * width)
        for k in range(4):
            d1 = lax.rem(me + k, 4)
            part = jnp.concatenate([ref[4 * r + d1] for r in range(4)], axis=0)
            if k == 0:
                own[:, at] = part
                source = own.at[:, at]
            else:
                code, value = code_of(part)
                coded[k - 1, :, at] = value.astype(jnp.int16)
                codes[k - 1] = jnp.where(lane == p, code, codes[k - 1])
                source = coded.at[k - 1, :, at]
            started.append(pltpu.make_async_copy(source, outs[k].at[:, at], o_sems.at[p, k]))
            started[-1].start()

    products = (even, odd)
    for p in range(number):
        if p in (0, split):
            for copy in (high if p else low):
                copy.wait()
        if p + 2 < number:
            for copy in fetch(p + 2):
                copy.start()
        for copy in fetch(p):
            copy.wait()
        left = lhs[p].reshape(4 * rows, depth)
        for side, at in ((0, core), (1, 1 - core)):
            at = pl.ds(pl.multiple_of(at * half, 128), half)
            products[p % 2][:, :, at] = pick(left, slots[p % 3, side]).reshape(16, 4 * m, half)
        if p > 0:
            finish(p - 1, products[(p - 1) % 2])
    finish(number - 1, products[(number - 1) % 2])
    at = slice(number * width, number * width + 128)
    for k in range(1, 4):
        coded[k - 1, :, at] = codes[k - 1].astype(jnp.int16)
        started.append(pltpu.make_async_copy(coded.at[k - 1, :, at], outs[k].at[:, at], o_sems.at[number, k]))
        started[-1].start()
    for copy in started:
        copy.wait()


def matmul(lows, highs, v_own, v_other, vir_counts, c_orbitals, m, start):
    c_dev, _, dmax, half = v_own.shape
    rows, depth, width = 16 * m, c_dev * dmax, 2 * half
    arrays = [a.reshape(-1, rows, depth) for a in lows + highs]
    number = arrays[0].shape[0] + arrays[-1].shape[0]
    shapes = [jax.ShapeDtypeStruct((rows, number * width), jnp.float32)]
    shapes += [jax.ShapeDtypeStruct((rows, number * width + 128), jnp.int16)] * 3
    return pl.pallas_call(
        functools.partial(matmul_kernel, m, start),
        in_specs=[SMEM] * 2 + [HBM] * 10,
        out_specs=[HBM] * 4,
        out_shape=shapes,
        scratch_shapes=[
            pltpu.VMEM((number, 4, rows, depth), jnp.bfloat16),
            pltpu.VMEM((3, 2, depth, half), jnp.bfloat16),
            pltpu.VMEM((16, 4 * m, width), jnp.float32),
            pltpu.VMEM((16, 4 * m, width), jnp.float32),
            pltpu.VMEM((rows, number * width), jnp.float32),
            pltpu.VMEM((3, rows, number * width + 128), jnp.int16),
            pltpu.VMEM((3, rows, 128), jnp.float32),
            pltpu.SemaphoreType.DMA((8,)),
            pltpu.SemaphoreType.DMA((3, 2, 8)),
            pltpu.SemaphoreType.DMA((number + 1, 4)),
        ],
        compiler_params=params(LIMIT),
        cost_estimate=cost(2 * number * 4 * rows * depth * width, number * v_own.size // 2),
    )(vir_counts, c_orbitals, *arrays, v_own, v_other)


def sum_kernel(number, own, q1, q2, q3, out, high, low):
    rows = own.shape[0]
    width = own.shape[1] // number
    lane = lax.broadcasted_iota(jnp.int32, (rows, 128), 1)
    scales = []
    for q in (q1, q2, q3):
        scales.append(jnp.exp2(q[:, number * width:].astype(jnp.float32) * (1.0 / FINE)) * (1.0 / TOP))
    for p in range(number):
        at = slice(p * width, (p + 1) * width)
        total = own[:, at]
        for q, scale in zip((q1, q2, q3), scales):
            one = jnp.sum(jnp.where(lane == p, scale, 0.0), axis=1, keepdims=True)
            total += q[:, at].astype(jnp.float32) * one
        code, value = code_of(total)
        value = jnp.concatenate([value, jnp.broadcast_to(code, (rows, 128))], axis=1)
        upper = jnp.round(value * (1.0 / 256.0))
        high[p * rows:(p + 1) * rows] = upper.astype(jnp.bfloat16)
        low[p * rows:(p + 1) * rows] = (value - 256.0 * upper).astype(jnp.bfloat16)
    order = one_hot(number * rows, lambda r: lax.rem(r, number) * rows + lax.div(r, number))
    out[...] = (pick(order, high[...]) * 256.0 + pick(order, low[...])).astype(jnp.int16)


def sum_coded(own, parts, number):
    rows, total = own.shape
    width = total // number + 128
    return pl.pallas_call(
        functools.partial(sum_kernel, number),
        in_specs=[VMEM] * 4,
        out_specs=VMEM,
        out_shape=jax.ShapeDtypeStruct((number * rows, width), jnp.int16),
        scratch_shapes=[pltpu.VMEM((number * rows, width), jnp.bfloat16)] * 2,
        compiler_params=params(LIMIT),
        cost_estimate=cost(8 * own.size, 12 * own.size),
    )(own, *parts)


def final_kernel(allow, *refs):
    got, out = refs[:-1], refs[-1]
    width = out.shape[1]
    pairs = out.shape[0] // 8
    start = 0
    for ref in got:
        number = ref.shape[0] // (4 * pairs)
        value = ref[...].astype(jnp.float32)
        scale = jnp.exp2(value[:, width:] * (1.0 / FINE)) * (1.0 / TOP)
        value = value[:, :width] * jnp.concatenate([scale] * (width // 128), axis=1)
        total = jnp.sum(value.reshape(4, pairs * number, width), axis=0)
        keep = allow[start:start + number] > 0.5
        for pair in range(pairs):
            part = total[pair * number:(pair + 1) * number]
            out[pair * 8 + start:pair * 8 + start + number] = jnp.where(keep, part, 0.0)
        start += number


def final(got, allow, pairs):
    width = got[0].shape[1] - 128
    return pl.pallas_call(
        final_kernel,
        grid=(4,),
        in_specs=[pl.BlockSpec((8, width), lambda i: (0, i))]
        + [pl.BlockSpec((g.shape[0] // 4, width + 128), lambda i: (i, 0)) for g in got],
        out_specs=pl.BlockSpec((8 * pairs, width), lambda i: (0, i)),
        out_shape=jax.ShapeDtypeStruct((8 * pairs, 4 * width), jnp.float32),
        compiler_params=params(LIMIT),
        cost_estimate=cost(10**7, 4 * 10**6),
    )(allow, *got)


def allowed(vir_counts, a_orbitals, dmax):
    labels = jnp.arange(8, dtype=jnp.int32)
    ends = jnp.sum(jnp.where(labels[:, None] <= labels[None, :], vir_counts[:, None], 0), axis=0)
    irrep = jnp.sum((a_orbitals[:, None] >= ends[None, :]).astype(jnp.int32), axis=1)
    block = jnp.bitwise_xor(labels[:, None], irrep[None, :])
    limit = jnp.sum(jnp.where(block[:, :, None] == labels, vir_counts, 0), axis=2)
    keep = jnp.arange(dmax, dtype=jnp.int32)[None, None, :] < limit[:, :, None]
    return keep.astype(jnp.float32).reshape(8, -1)


def shards(amplitudes, integrals, vir_counts, c_orbitals, a_orbitals):
    m, irreps, c_tot, dmax = amplitudes.shape
    depth = c_tot // 16 * dmax
    other = send(integrals, SWAP)
    core = lax.axis_index("pair") % 2
    by_s = jnp.swapaxes(amplitudes, 2, 3)
    starts = [sum(SPLIT[:i]) for i in range(len(SPLIT))]
    pieces = [arrange(by_s, vir_counts, c_orbitals, s, n) for s, n in zip(starts, SPLIT)]

    relaid = []
    for chunk, number in enumerate(SPLIT):
        size = 16 * m * number
        r = jnp.arange(size, dtype=jnp.int32)
        minor, d2, d1, label = r % m, r // m % 4, r // (4 * m) % 4, r // (16 * m)
        dy = jnp.where(core == 0, d1, d2)
        dz = jnp.where(core == 0, d2, d1)
        source = ((dz * 4 + dy) * m + minor) * number + label
        chooser = (source[:, None] == r[None, :]).astype(jnp.bfloat16)
        piece = pieces[chunk].reshape(16, m * number, depth)
        got = lax.all_to_all(piece, "slab", split_axis=0, concat_axis=0, tiled=True).reshape(size, depth)
        if chunk == 0:
            got, *pieces[1:] = lax.optimization_barrier((got, *pieces[1:]))
        cut = size // 2
        relaid.append([pick(part, got).astype(jnp.bfloat16) for part in (chooser[:cut], chooser[cut:])])

    products, before = [], None
    for chunk, (low, high) in enumerate(relaid):
        if before is not None:
            low, high, *_ = lax.optimization_barrier((low, high, *before))
        low1, high3 = send(low, X_DOWN), send(high, X_UP)
        high1, low3 = send(high, X_DOWN), send(low, X_UP)
        if products:
            low1, high3, _ = lax.optimization_barrier((low1, high3, products[-1][0]))
        low2, high2 = send(low1, X_DOWN), send(high3, X_UP)
        before = (low2, high2)
        arrays = [low, low1, low2, low3, high, high1, high2, high3]
        if chunk + 1 < len(SPLIT):
            arrays = lax.optimization_barrier((*arrays, *relaid[chunk + 1]))
            relaid[chunk + 1] = arrays[8:]
        products.append(matmul(
            list(arrays[:4]), list(arrays[4:8]), integrals, other, vir_counts, c_orbitals, m, starts[chunk]
        ))

    sent = [[send(q, first(k)) for k, q in enumerate(product) if k] for product in products]
    results = []
    for chunk, number in enumerate(SPLIT):
        own, parts = products[chunk][0], sent[chunk]
        if chunk + 1 < len(SPLIT):
            own, *parts = lax.optimization_barrier((own, *parts, products[chunk + 1][0]))[:4]
        coded = sum_coded(own, parts, number)
        coded = coded.reshape(16, m * number, coded.shape[1])
        got = lax.all_to_all(coded, AXES, split_axis=0, concat_axis=0, tiled=True, axis_index_groups=GROUPS)
        results.append(got.reshape(16 * m * number, got.shape[2]))
    full = final(results, allowed(vir_counts, a_orbitals, dmax), m)
    return full.reshape(m, irreps, full.shape[1])


def solution(mesh):
    in_specs = (P(("pair", "slab"), None, None, None), P("slab", None, None, "pair"), P(), P(), P())
    out_specs = P(("pair", "slab"), None, None)
    return jax.shard_map(shards, mesh=mesh, in_specs=in_specs, out_specs=out_specs, check_vma=False)
```

```python
import functools

import jax
import jax.numpy as jnp
from jax import lax
from jax.experimental import pallas as pl
from jax.experimental.pallas import tpu as pltpu
from jax.sharding import PartitionSpec as P

SPLIT = (4, 4)
TOP = 32766.0
FINE = 256.0
AXES = ("slab", "pair")
MIB = 2**20
LIMIT = 52
HBM = pl.BlockSpec(memory_space=pl.ANY)
VMEM = pl.BlockSpec(memory_space=pltpu.VMEM)
SMEM = pl.BlockSpec(memory_space=pltpu.SMEM)


def place(z, y, x, core):
    return ((z % 4) * 4 + y % 4) * 8 + (x % 4) * 2 + core


def moves(target):
    return [
        (place(z, y, x, core), place(*target(z, y, x, core)))
        for z in range(4) for y in range(4) for x in range(4) for core in range(2)
    ]


X_UP = moves(lambda z, y, x, core: (z, y, x + 1, core))
X_DOWN = moves(lambda z, y, x, core: (z, y, x - 1, core))
SWAP = moves(lambda z, y, x, core: (z, y, x, 1 - core))
GROUPS = [[place(z, y, x, 0) for x in range(4) for z in range(4)] for y in range(4)]
GROUPS += [[place(z, y, x, 1) for x in range(4) for y in range(4)] for z in range(4)]


def first(k):
    return moves(lambda z, y, x, core: (z, y + k, x, core) if core == 0 else (z + k, y, x, core))


def send(value, pairs):
    return lax.ppermute(value, AXES, pairs)


def in_vmem(values):
    return [pltpu.with_memory_space_constraint(v, pltpu.VMEM) for v in values]


def cost(flops, size):
    return pl.CostEstimate(flops=flops, bytes_accessed=size, transcendentals=0)


def params(size):
    return pltpu.CompilerParams(vmem_limit_bytes=size * MIB)


def one_hot(rows, source):
    r = lax.broadcasted_iota(jnp.int32, (rows, rows), 0)
    col = lax.broadcasted_iota(jnp.int32, (rows, rows), 1)
    return (source(r) == col).astype(jnp.float32).astype(jnp.bfloat16)


def pick(matrix, value):
    return jnp.dot(matrix, value, preferred_element_type=jnp.float32)


def code_of(part):
    peak = jnp.maximum(jnp.max(jnp.abs(part), axis=1, keepdims=True), 2.0**-100)
    code = jnp.ceil(jnp.log2(peak) * FINE)
    return code, jnp.round(part * (jnp.exp2(code * (-1.0 / FINE)) * TOP))


def ends_of(counts):
    ends, total = [], 0
    for g in range(8):
        total = total + counts[g]
        ends.append(total)
    return ends


def arrange_kernel(start, count, counts, c_ref, t_ref, out, sorted_ref):
    pairs, _, dmax, c_tot = t_ref.shape
    n_slab = c_tot // 8
    rows = pairs * count
    ends = ends_of(counts)
    orbital = c_ref[...]
    irrep = sum((orbital >= ends[g]).astype(jnp.int32) for g in range(8))
    slot = lax.broadcasted_iota(jnp.int32, (dmax, c_tot), 0)
    by_c = one_hot(c_tot, lambda r: lax.rem(r, n_slab) * 8 + lax.div(r, n_slab))
    for p in range(count):
        block = jnp.bitwise_xor(irrep, start + p)
        limit = sum(jnp.where(block == g, counts[g], 0) for g in range(8))
        keep = slot < limit
        for pair in range(pairs):
            kept = jnp.where(keep, t_ref[pair, start + p].astype(jnp.float32), 0.0).astype(jnp.bfloat16)
            split = lax.dot_general(by_c, kept, (((1,), (1,)), ((), ())), preferred_element_type=jnp.float32)
            split = split.astype(jnp.bfloat16)
            q = pair * count + p
            for c in range(8):
                sorted_ref[c, q * n_slab:(q + 1) * n_slab] = split[c * n_slab:(c + 1) * n_slab]
    by_slab = one_hot(n_slab * rows, lambda r: lax.rem(r, rows) * n_slab + lax.div(r, rows))
    for i in range(4):
        both = [pick(by_slab, sorted_ref[2 * i + h]) for h in range(2)]
        out[:, i * 2 * dmax:(i + 1) * 2 * dmax] = jnp.concatenate(both, axis=1).astype(jnp.bfloat16)


def arrange(amplitudes, vir_counts, c_orbitals, start, count):
    rows, _, dmax, c_tot = amplitudes.shape
    size = c_tot // 8 * rows * count
    return pl.pallas_call(
        functools.partial(arrange_kernel, start, count),
        grid=(1,),
        in_specs=[
            SMEM,
            pl.BlockSpec((1, c_tot), lambda i: (0, 0)),
            pl.BlockSpec((rows, 8, dmax, c_tot), lambda i: (0, 0, 0, 0)),
        ],
        out_specs=pl.BlockSpec((size, 8 * dmax), lambda i: (0, 0)),
        out_shape=jax.ShapeDtypeStruct((size, 8 * dmax), jnp.bfloat16),
        scratch_shapes=[pltpu.VMEM((8, size, dmax), jnp.bfloat16)],
        compiler_params=params(58),
        cost_estimate=cost(2 * 10**9, 4 * 10**6),
    )(vir_counts, c_orbitals.reshape(1, c_tot), amplitudes)


def copies_of(sides, counts, c_orbitals, label, target, sems):
    c_dev, _, dmax, _ = sides[0].shape
    ends = ends_of(counts)
    slab = lax.axis_index("slab")
    copies = []
    for c in range(c_dev):
        orbital = c_orbitals[slab * c_dev + c]
        irrep = sum((orbital >= ends[g]).astype(jnp.int32) for g in range(8))
        for side, ref in enumerate(sides):
            copies.append(pltpu.make_async_copy(
                ref.at[c, jnp.bitwise_xor(irrep, label)], target.at[side, pl.ds(c * dmax, dmax)], sems.at[side, c]
            ))
    return copies


def load_kernel(label, counts, c_orbitals, v_own, v_other, after, out, sems):
    del after
    copies = copies_of((v_own, v_other), counts, c_orbitals, label, out, sems)
    for copy in copies:
        copy.start()
    for copy in copies:
        copy.wait()


def load(v_own, v_other, vir_counts, c_orbitals, label, after):
    c_dev, _, dmax, half = v_own.shape
    return pl.pallas_call(
        functools.partial(load_kernel, label),
        in_specs=[SMEM, SMEM, HBM, HBM, HBM],
        out_specs=VMEM,
        out_shape=pltpu.VMEM((2, c_dev * dmax, half), jnp.bfloat16),
        scratch_shapes=[pltpu.SemaphoreType.DMA((2, c_dev))],
        compiler_params=params(LIMIT),
        cost_estimate=cost(0, v_own.size),
    )(vir_counts, c_orbitals, v_own, v_other, after)


def matmul_kernel(m, start, counts, c_orbitals, *refs):
    lows, highs, sides = refs[:4], refs[4:8], refs[8:10]
    ready = refs[10]
    outs = refs[-14:-10]
    lhs, slots, even, odd, own, coded, codes, sems, v_sems, o_sems = refs[-10:]
    number, _, rows, depth = lhs.shape
    half = sides[0].shape[3]
    width = 2 * half
    split = lows[0].shape[0]
    slab, pair = lax.axis_index("slab"), lax.axis_index("pair")
    x, core = lax.div(pair, 2), lax.rem(pair, 2)
    me = jnp.where(core == 0, lax.rem(slab, 4), lax.div(slab, 4))

    def fetch(p):
        if p == 0:
            return []
        return copies_of(sides, counts, c_orbitals, start + p, slots.at[p % 3], v_sems.at[p % 3])

    def arrivals(refs, first_p, at):
        return [
            pltpu.make_async_copy(ref, lhs.at[pl.ds(first_p, ref.shape[0]), lax.rem(x + r, 4)], sems.at[at + r])
            for r, ref in enumerate(refs)
        ]

    low, high = arrivals(lows, 0, 0), arrivals(highs, split, 4)
    for copy in low + fetch(0) + high + fetch(1):
        copy.start()
    codes[...] = jnp.zeros_like(codes)
    lane = lax.broadcasted_iota(jnp.int32, (rows, 128), 1)
    started = []

    def finish(p, ref):
        at = slice(p * width, (p + 1) * width)
        for k in range(4):
            d1 = lax.rem(me + k, 4)
            part = jnp.concatenate([ref[4 * r + d1] for r in range(4)], axis=0)
            if k == 0:
                own[:, at] = part
                source = own.at[:, at]
            else:
                code, value = code_of(part)
                coded[k - 1, :, at] = value.astype(jnp.int16)
                codes[k - 1] = jnp.where(lane == p, code, codes[k - 1])
                source = coded.at[k - 1, :, at]
            started.append(pltpu.make_async_copy(source, outs[k].at[:, at], o_sems.at[p, k]))
            started[-1].start()

    products = (even, odd)
    for p in range(number):
        if p in (0, split):
            for copy in (high if p else low):
                copy.wait()
        if p + 2 < number:
            for copy in fetch(p + 2):
                copy.start()
        for copy in fetch(p):
            copy.wait()
        left = lhs[p].reshape(4 * rows, depth)
        for side, at in ((0, core), (1, 1 - core)):
            at = pl.ds(pl.multiple_of(at * half, 128), half)
            right = slots[p % 3, side] if p else ready[side]
            products[p % 2][:, :, at] = pick(left, right).reshape(16, 4 * m, half)
        if p > 0:
            finish(p - 1, products[(p - 1) % 2])
    finish(number - 1, products[(number - 1) % 2])
    at = slice(number * width, number * width + 128)
    for k in range(1, 4):
        coded[k - 1, :, at] = codes[k - 1].astype(jnp.int16)
        started.append(pltpu.make_async_copy(coded.at[k - 1, :, at], outs[k].at[:, at], o_sems.at[number, k]))
        started[-1].start()
    for copy in started:
        copy.wait()


def matmul(lows, highs, v_own, v_other, vir_counts, c_orbitals, m, start, ready, near):
    c_dev, _, dmax, half = v_own.shape
    rows, depth, width = 16 * m, c_dev * dmax, 2 * half
    arrays = [a.reshape(-1, rows, depth) for a in lows + highs]
    number = arrays[0].shape[0] + arrays[-1].shape[0]
    shapes = [jax.ShapeDtypeStruct((rows, number * width), jnp.float32)]
    shapes += [jax.ShapeDtypeStruct((rows, number * width + 128), jnp.int16)] * 3
    if near:
        arrays = in_vmem(arrays)
    return pl.pallas_call(
        functools.partial(matmul_kernel, m, start),
        in_specs=[SMEM] * 2 + [VMEM if near else HBM] * 8 + [HBM] * 2 + [VMEM],
        out_specs=[HBM] * 4,
        out_shape=shapes,
        scratch_shapes=[
            pltpu.VMEM((number, 4, rows, depth), jnp.bfloat16),
            pltpu.VMEM((3, 2, depth, half), jnp.bfloat16),
            pltpu.VMEM((16, 4 * m, width), jnp.float32),
            pltpu.VMEM((16, 4 * m, width), jnp.float32),
            pltpu.VMEM((rows, number * width), jnp.float32),
            pltpu.VMEM((3, rows, number * width + 128), jnp.int16),
            pltpu.VMEM((3, rows, 128), jnp.float32),
            pltpu.SemaphoreType.DMA((8,)),
            pltpu.SemaphoreType.DMA((3, 2, 8)),
            pltpu.SemaphoreType.DMA((number + 1, 4)),
        ],
        compiler_params=params(LIMIT),
        cost_estimate=cost(2 * number * 4 * rows * depth * width, number * v_own.size // 2),
    )(vir_counts, c_orbitals, *arrays, v_own, v_other, *in_vmem([ready]))


def sum_kernel(number, own_ref, q1, q2, q3, out, own, q, high, low, sems):
    rows = own.shape[0]
    width = own.shape[1] // number
    tail = slice(number * width, number * width + 128)
    codes = [pltpu.make_async_copy(ref.at[:, tail], q.at[k, :, tail], sems.at[number, k]) for k, ref in enumerate((q1, q2, q3))]
    copies = []
    for p in range(number):
        at = slice(p * width, (p + 1) * width)
        copies.append([pltpu.make_async_copy(own_ref.at[:, at], own.at[:, at], sems.at[p, 3])])
        for k, ref in enumerate((q1, q2, q3)):
            copies[p].append(pltpu.make_async_copy(ref.at[:, at], q.at[k, :, at], sems.at[p, k]))
    for group in [codes] + copies:
        for copy in group:
            copy.start()
    lane = lax.broadcasted_iota(jnp.int32, (rows, 128), 1)
    for copy in codes:
        copy.wait()
    scales = [jnp.exp2(q[k, :, tail].astype(jnp.float32) * (1.0 / FINE)) * (1.0 / TOP) for k in range(3)]
    for p in range(number):
        for copy in copies[p]:
            copy.wait()
        at = slice(p * width, (p + 1) * width)
        total = own[:, at]
        for k in range(3):
            one = jnp.sum(jnp.where(lane == p, scales[k], 0.0), axis=1, keepdims=True)
            total += q[k, :, at].astype(jnp.float32) * one
        code, value = code_of(total)
        value = jnp.concatenate([value, jnp.broadcast_to(code, (rows, 128))], axis=1)
        upper = jnp.round(value * (1.0 / 256.0))
        high[p * rows:(p + 1) * rows] = upper.astype(jnp.bfloat16)
        low[p * rows:(p + 1) * rows] = (value - 256.0 * upper).astype(jnp.bfloat16)
    order = one_hot(number * rows, lambda r: lax.rem(r, number) * rows + lax.div(r, number))
    out[...] = (pick(order, high[...]) * 256.0 + pick(order, low[...])).astype(jnp.int16)


def sum_coded(own, parts, number):
    rows, total = own.shape
    width = total // number + 128
    return pl.pallas_call(
        functools.partial(sum_kernel, number),
        in_specs=[HBM] * 4,
        out_specs=VMEM,
        out_shape=jax.ShapeDtypeStruct((number * rows, width), jnp.int16),
        scratch_shapes=[
            pltpu.VMEM(own.shape, jnp.float32),
            pltpu.VMEM((3,) + parts[0].shape, jnp.int16),
            pltpu.VMEM((number * rows, width), jnp.bfloat16),
            pltpu.VMEM((number * rows, width), jnp.bfloat16),
            pltpu.SemaphoreType.DMA((number + 1, 4)),
        ],
        compiler_params=params(LIMIT),
        cost_estimate=cost(8 * own.size, 12 * own.size),
    )(own, *parts)


def final_kernel(allow, *refs):
    got, out = refs[:-1], refs[-1]
    width = out.shape[1] // 4
    pairs = out.shape[0] // 8
    for x in range(4):
        start = 0
        for ref in got:
            number = ref.shape[0] // (16 * pairs)
            total = 0.0
            size = pairs * number
            for d2 in range(4):
                value = ref[(4 * x + d2) * size:(4 * x + d2 + 1) * size].astype(jnp.float32)
                scale = jnp.exp2(value[:, width:] * (1.0 / FINE)) * (1.0 / TOP)
                total += value[:, :width] * jnp.concatenate([scale] * (width // 128), axis=1)
            at = slice(x * width, (x + 1) * width)
            keep = allow[start:start + number, at] > 0.5
            for pair in range(pairs):
                part = total[pair * number:(pair + 1) * number]
                out[pair * 8 + start:pair * 8 + start + number, at] = jnp.where(keep, part, 0.0)
            start += number


def final(got, allow, pairs):
    width = got[0].shape[1] - 128
    last = pltpu.with_memory_space_constraint(got[-1], pltpu.VMEM)
    return pl.pallas_call(
        final_kernel,
        in_specs=[VMEM] * (1 + len(got)),
        out_specs=VMEM,
        out_shape=jax.ShapeDtypeStruct((8 * pairs, 4 * width), jnp.float32),
        compiler_params=params(24),
        cost_estimate=cost(10**7, 4 * 10**6),
    )(allow, *got[:-1], last)


def allowed(vir_counts, a_orbitals, dmax):
    labels = jnp.arange(8, dtype=jnp.int32)
    ends = jnp.sum(jnp.where(labels[:, None] <= labels[None, :], vir_counts[:, None], 0), axis=0)
    irrep = jnp.sum((a_orbitals[:, None] >= ends[None, :]).astype(jnp.int32), axis=1)
    block = jnp.bitwise_xor(labels[:, None], irrep[None, :])
    limit = jnp.sum(jnp.where(block[:, :, None] == labels, vir_counts, 0), axis=2)
    keep = jnp.arange(dmax, dtype=jnp.int32)[None, None, :] < limit[:, :, None]
    return keep.astype(jnp.float32).reshape(8, -1)


def shards(amplitudes, integrals, vir_counts, c_orbitals, a_orbitals):
    m, irreps, c_tot, dmax = amplitudes.shape
    depth = c_tot // 16 * dmax
    other = send(integrals, SWAP)
    core = lax.axis_index("pair") % 2
    by_s = jnp.swapaxes(amplitudes, 2, 3)
    starts = [sum(SPLIT[:i]) for i in range(len(SPLIT))]
    pieces = [arrange(by_s, vir_counts, c_orbitals, s, n) for s, n in zip(starts, SPLIT)]

    relaid = []
    for chunk, number in enumerate(SPLIT):
        size = 16 * m * number
        r = jnp.arange(size, dtype=jnp.int32)
        minor, d2, d1, label = r % m, r // m % 4, r // (4 * m) % 4, r // (16 * m)
        dy = jnp.where(core == 0, d1, d2)
        dz = jnp.where(core == 0, d2, d1)
        source = ((dz * 4 + dy) * m + minor) * number + label
        chooser = (source[:, None] == r[None, :]).astype(jnp.bfloat16)
        piece = pieces[chunk].reshape(16, m * number, depth)
        got = lax.all_to_all(piece, "slab", split_axis=0, concat_axis=0, tiled=True).reshape(size, depth)
        if chunk == 0:
            got, *pieces[1:] = lax.optimization_barrier((got, *pieces[1:]))
        cut = 16 * m * (number // 2)
        relaid.append([pick(part, got).astype(jnp.bfloat16) for part in (chooser[:cut], chooser[cut:])])

    products, before = [], None
    for chunk, (low, high) in enumerate(relaid):
        if before is not None:
            low, high, other, *_ = lax.optimization_barrier((low, high, other, *before))
        low1, high3 = send(low, X_DOWN), send(high, X_UP)
        high1, low3 = send(high, X_DOWN), send(low, X_UP)
        before = (high1, low3)
        if products:
            low1, high3, _ = lax.optimization_barrier((low1, high3, products[-1][0]))
        low2, high2 = send(low1, X_DOWN), send(high3, X_UP)
        arrays = [low, low1, low2, low3, high, high1, high2, high3]
        operands = (integrals, other, vir_counts, c_orbitals)
        ready = load(*operands, starts[chunk], products[-1][1] if chunk else relaid[-1][0])
        products.append(matmul(arrays[:4], arrays[4:], *operands, m, starts[chunk], ready, chunk > 0))

    sent = [[send(q, first(k)) for k, q in enumerate(product) if k] for product in products]
    results = []
    for chunk, number in enumerate(SPLIT):
        own, parts = products[chunk][0], sent[chunk]
        if chunk + 1 < len(SPLIT):
            own, *parts = lax.optimization_barrier((own, *parts, products[chunk + 1][0]))[:4]
        coded = sum_coded(own, parts, number)
        coded = coded.reshape(16, m * number, coded.shape[1])
        got = lax.all_to_all(coded, AXES, split_axis=0, concat_axis=0, tiled=True, axis_index_groups=GROUPS)
        results.append(got.reshape(16 * m * number, got.shape[2]))
    full = final(results, allowed(vir_counts, a_orbitals, dmax), m)
    return full.reshape(m, irreps, full.shape[1])


def solution(mesh):
    in_specs = (P(("pair", "slab"), None, None, None), P("slab", None, None, "pair"), P(), P(), P())
    out_specs = P(("pair", "slab"), None, None)
    return jax.shard_map(shards, mesh=mesh, in_specs=in_specs, out_specs=out_specs, check_vma=False)
```

```python
import functools

import jax
import jax.numpy as jnp
from jax import lax
from jax.experimental import pallas as pl
from jax.experimental.pallas import tpu as pltpu
from jax.sharding import PartitionSpec as P

SPLIT = (4, 4)
TOP = 32766.0
FINE = 256.0
AXES = ("slab", "pair")
MIB = 2**20
LIMIT = 52
HBM = pl.BlockSpec(memory_space=pl.ANY)
VMEM = pl.BlockSpec(memory_space=pltpu.VMEM)
SMEM = pl.BlockSpec(memory_space=pltpu.SMEM)


def place(z, y, x, core):
    return ((z % 4) * 4 + y % 4) * 8 + (x % 4) * 2 + core


def moves(target):
    return [
        (place(z, y, x, core), place(*target(z, y, x, core)))
        for z in range(4) for y in range(4) for x in range(4) for core in range(2)
    ]


X_UP = moves(lambda z, y, x, core: (z, y, x + 1, core))
X_DOWN = moves(lambda z, y, x, core: (z, y, x - 1, core))
SWAP = moves(lambda z, y, x, core: (z, y, x, 1 - core))
GROUPS = [[place(z, y, x, 0) for x in range(4) for z in range(4)] for y in range(4)]
GROUPS += [[place(z, y, x, 1) for x in range(4) for y in range(4)] for z in range(4)]


def first(k):
    return moves(lambda z, y, x, core: (z, y + k, x, core) if core == 0 else (z + k, y, x, core))


def send(value, pairs):
    return lax.ppermute(value, AXES, pairs)


def in_vmem(values):
    return [pltpu.with_memory_space_constraint(v, pltpu.VMEM) for v in values]


def cost(flops, size):
    return pl.CostEstimate(flops=flops, bytes_accessed=size, transcendentals=0)


def params(size):
    return pltpu.CompilerParams(vmem_limit_bytes=size * MIB)


def one_hot(rows, source):
    r = lax.broadcasted_iota(jnp.int32, (rows, rows), 0)
    col = lax.broadcasted_iota(jnp.int32, (rows, rows), 1)
    return (source(r) == col).astype(jnp.float32).astype(jnp.bfloat16)


def pick(matrix, value):
    return jnp.dot(matrix, value, preferred_element_type=jnp.float32)


def code_of(part):
    peak = jnp.maximum(jnp.max(jnp.abs(part), axis=1, keepdims=True), 2.0**-100)
    code = jnp.ceil(jnp.log2(peak) * FINE)
    return code, jnp.round(part * (jnp.exp2(code * (-1.0 / FINE)) * TOP))


def ends_of(counts):
    ends, total = [], 0
    for g in range(8):
        total = total + counts[g]
        ends.append(total)
    return ends


def arrange_kernel(start, count, counts, c_ref, t_ref, out, sorted_ref):
    pairs, _, dmax, c_tot = t_ref.shape
    n_slab = c_tot // 8
    rows = pairs * count
    ends = ends_of(counts)
    orbital = c_ref[...]
    irrep = sum((orbital >= ends[g]).astype(jnp.int32) for g in range(8))
    slot = lax.broadcasted_iota(jnp.int32, (dmax, c_tot), 0)
    by_c = one_hot(c_tot, lambda r: lax.rem(r, n_slab) * 8 + lax.div(r, n_slab))
    for p in range(count):
        block = jnp.bitwise_xor(irrep, start + p)
        limit = sum(jnp.where(block == g, counts[g], 0) for g in range(8))
        keep = slot < limit
        for pair in range(pairs):
            kept = jnp.where(keep, t_ref[pair, p].astype(jnp.float32), 0.0).astype(jnp.bfloat16)
            split = lax.dot_general(by_c, kept, (((1,), (1,)), ((), ())), preferred_element_type=jnp.float32)
            split = split.astype(jnp.bfloat16)
            q = pair * count + p
            for c in range(8):
                sorted_ref[c, q * n_slab:(q + 1) * n_slab] = split[c * n_slab:(c + 1) * n_slab]
    by_slab = one_hot(n_slab * rows, lambda r: lax.rem(r, rows) * n_slab + lax.div(r, rows))
    for i in range(4):
        both = [pick(by_slab, sorted_ref[2 * i + h]) for h in range(2)]
        out[:, i * 2 * dmax:(i + 1) * 2 * dmax] = jnp.concatenate(both, axis=1).astype(jnp.bfloat16)


def arrange(amplitudes, vir_counts, c_orbitals, start, count):
    rows, _, dmax, c_tot = amplitudes.shape
    size = c_tot // 8 * rows * count
    return pl.pallas_call(
        functools.partial(arrange_kernel, start, count),
        grid=(1,),
        in_specs=[
            SMEM,
            pl.BlockSpec((1, c_tot), lambda i: (0, 0)),
            pl.BlockSpec((rows, count, dmax, c_tot), lambda i: (0, start // count, 0, 0)),
        ],
        out_specs=pl.BlockSpec((size, 8 * dmax), lambda i: (0, 0)),
        out_shape=jax.ShapeDtypeStruct((size, 8 * dmax), jnp.bfloat16),
        scratch_shapes=[pltpu.VMEM((8, size, dmax), jnp.bfloat16)],
        compiler_params=params(58),
        cost_estimate=cost(2 * 10**9, 4 * 10**6),
    )(vir_counts, c_orbitals.reshape(1, c_tot), amplitudes)


def copies_of(sides, counts, c_orbitals, label, target, sems):
    c_dev, _, dmax, _ = sides[0].shape
    ends = ends_of(counts)
    slab = lax.axis_index("slab")
    copies = []
    for c in range(c_dev):
        orbital = c_orbitals[slab * c_dev + c]
        irrep = sum((orbital >= ends[g]).astype(jnp.int32) for g in range(8))
        for side, ref in enumerate(sides):
            copies.append(pltpu.make_async_copy(
                ref.at[c, jnp.bitwise_xor(irrep, label)], target.at[side, pl.ds(c * dmax, dmax)], sems.at[side, c]
            ))
    return copies


def load_kernel(label, counts, c_orbitals, v_own, v_other, after, out, sems):
    del after
    copies = copies_of((v_own, v_other), counts, c_orbitals, label, out, sems)
    for copy in copies:
        copy.start()
    for copy in copies:
        copy.wait()


def load(v_own, v_other, vir_counts, c_orbitals, label, after):
    c_dev, _, dmax, half = v_own.shape
    return pl.pallas_call(
        functools.partial(load_kernel, label),
        in_specs=[SMEM, SMEM, HBM, HBM, HBM],
        out_specs=VMEM,
        out_shape=pltpu.VMEM((2, c_dev * dmax, half), jnp.bfloat16),
        scratch_shapes=[pltpu.SemaphoreType.DMA((2, c_dev))],
        compiler_params=params(LIMIT),
        cost_estimate=cost(0, v_own.size),
    )(vir_counts, c_orbitals, v_own, v_other, after)


def matmul_kernel(m, start, counts, c_orbitals, *refs):
    lows, highs, sides = refs[:4], refs[4:8], refs[8:10]
    ready = refs[10]
    outs = refs[-14:-10]
    lhs, slots, even, odd, own, coded, codes, sems, v_sems, o_sems = refs[-10:]
    number, _, rows, depth = lhs.shape
    half = sides[0].shape[3]
    width = 2 * half
    split = lows[0].shape[0]
    slab, pair = lax.axis_index("slab"), lax.axis_index("pair")
    x, core = lax.div(pair, 2), lax.rem(pair, 2)
    me = jnp.where(core == 0, lax.rem(slab, 4), lax.div(slab, 4))

    def fetch(p):
        if p == 0:
            return []
        return copies_of(sides, counts, c_orbitals, start + p, slots.at[p % 3], v_sems.at[p % 3])

    def arrivals(refs, first_p, at):
        return [
            pltpu.make_async_copy(ref, lhs.at[pl.ds(first_p, ref.shape[0]), lax.rem(x + r, 4)], sems.at[at + r])
            for r, ref in enumerate(refs)
        ]

    low, high = arrivals(lows, 0, 0), arrivals(highs, split, 4)
    for copy in low + fetch(0) + high + fetch(1):
        copy.start()
    codes[...] = jnp.zeros_like(codes)
    lane = lax.broadcasted_iota(jnp.int32, (rows, 128), 1)
    started = []

    def finish(p, ref):
        at = slice(p * width, (p + 1) * width)
        for k in range(4):
            d1 = lax.rem(me + k, 4)
            part = jnp.concatenate([ref[4 * r + d1] for r in range(4)], axis=0)
            if k == 0:
                own[:, at] = part
                source = own.at[:, at]
            else:
                code, value = code_of(part)
                coded[k - 1, :, at] = value.astype(jnp.int16)
                codes[k - 1] = jnp.where(lane == p, code, codes[k - 1])
                source = coded.at[k - 1, :, at]
            started.append(pltpu.make_async_copy(source, outs[k].at[:, at], o_sems.at[p, k]))
            started[-1].start()

    products = (even, odd)
    for p in range(number):
        if p in (0, split):
            for copy in (high if p else low):
                copy.wait()
        if p + 2 < number:
            for copy in fetch(p + 2):
                copy.start()
        for copy in fetch(p):
            copy.wait()
        left = lhs[p].reshape(4 * rows, depth)
        for side, at in ((0, core), (1, 1 - core)):
            at = pl.ds(pl.multiple_of(at * half, 128), half)
            right = slots[p % 3, side] if p else ready[side]
            products[p % 2][:, :, at] = pick(left, right).reshape(16, 4 * m, half)
        if p > 0:
            finish(p - 1, products[(p - 1) % 2])
    finish(number - 1, products[(number - 1) % 2])
    at = slice(number * width, number * width + 128)
    for k in range(1, 4):
        coded[k - 1, :, at] = codes[k - 1].astype(jnp.int16)
        started.append(pltpu.make_async_copy(coded.at[k - 1, :, at], outs[k].at[:, at], o_sems.at[number, k]))
        started[-1].start()
    for copy in started:
        copy.wait()


def matmul(lows, highs, v_own, v_other, vir_counts, c_orbitals, m, start, ready, near):
    c_dev, _, dmax, half = v_own.shape
    rows, depth, width = 16 * m, c_dev * dmax, 2 * half
    arrays = [a.reshape(-1, rows, depth) for a in lows + highs]
    number = arrays[0].shape[0] + arrays[-1].shape[0]
    shapes = [jax.ShapeDtypeStruct((rows, number * width), jnp.float32)]
    shapes += [jax.ShapeDtypeStruct((rows, number * width + 128), jnp.int16)] * 3
    if near:
        arrays = in_vmem(arrays)
    return pl.pallas_call(
        functools.partial(matmul_kernel, m, start),
        in_specs=[SMEM] * 2 + [VMEM if near else HBM] * 8 + [HBM] * 2 + [VMEM],
        out_specs=[HBM] * 4,
        out_shape=shapes,
        scratch_shapes=[
            pltpu.VMEM((number, 4, rows, depth), jnp.bfloat16),
            pltpu.VMEM((3, 2, depth, half), jnp.bfloat16),
            pltpu.VMEM((16, 4 * m, width), jnp.float32),
            pltpu.VMEM((16, 4 * m, width), jnp.float32),
            pltpu.VMEM((rows, number * width), jnp.float32),
            pltpu.VMEM((3, rows, number * width + 128), jnp.int16),
            pltpu.VMEM((3, rows, 128), jnp.float32),
            pltpu.SemaphoreType.DMA((8,)),
            pltpu.SemaphoreType.DMA((3, 2, 8)),
            pltpu.SemaphoreType.DMA((number + 1, 4)),
        ],
        compiler_params=params(LIMIT),
        cost_estimate=cost(2 * number * 4 * rows * depth * width, number * v_own.size // 2),
    )(vir_counts, c_orbitals, *arrays, v_own, v_other, *in_vmem([ready]))


def sum_kernel(number, own_ref, q1, q2, q3, out, own, q, mixed, sems):
    rows = own.shape[0]
    width = own.shape[1] // number
    tail = slice(number * width, number * width + 128)
    codes = [pltpu.make_async_copy(ref.at[:, tail], q.at[k, :, tail], sems.at[number, k]) for k, ref in enumerate((q1, q2, q3))]
    copies = []
    for p in range(number):
        at = slice(p * width, (p + 1) * width)
        copies.append([pltpu.make_async_copy(own_ref.at[:, at], own.at[:, at], sems.at[p, 3])])
        for k, ref in enumerate((q1, q2, q3)):
            copies[p].append(pltpu.make_async_copy(ref.at[:, at], q.at[k, :, at], sems.at[p, k]))
    for group in [codes] + copies:
        for copy in group:
            copy.start()
    lane = lax.broadcasted_iota(jnp.int32, (rows, 128), 1)
    for copy in codes:
        copy.wait()
    scales = [jnp.exp2(q[k, :, tail].astype(jnp.float32) * (1.0 / FINE)) * (1.0 / TOP) for k in range(3)]
    for p in range(number):
        for copy in copies[p]:
            copy.wait()
        at = slice(p * width, (p + 1) * width)
        total = own[:, at]
        for k in range(3):
            one = jnp.sum(jnp.where(lane == p, scales[k], 0.0), axis=1, keepdims=True)
            total += q[k, :, at].astype(jnp.float32) * one
        code, value = code_of(total)
        value = jnp.concatenate([value, jnp.broadcast_to(code, (rows, 128))], axis=1)
        for j in range(mixed.shape[0]):
            mixed[j, pl.ds(p, rows, number), :] = value[:, j * 128:(j + 1) * 128]
    for j in range(mixed.shape[0]):
        out[:, j * 128:(j + 1) * 128] = mixed[j].astype(jnp.int16)


def sum_coded(own, parts, number):
    rows, total = own.shape
    width = total // number + 128
    return pl.pallas_call(
        functools.partial(sum_kernel, number),
        in_specs=[HBM] * 4,
        out_specs=VMEM,
        out_shape=jax.ShapeDtypeStruct((number * rows, width), jnp.int16),
        scratch_shapes=[
            pltpu.VMEM(own.shape, jnp.float32),
            pltpu.VMEM((3,) + parts[0].shape, jnp.int16),
            pltpu.VMEM((width // 128, number * rows, 128), jnp.float32),
            pltpu.SemaphoreType.DMA((number + 1, 4)),
        ],
        compiler_params=params(LIMIT),
        cost_estimate=cost(8 * own.size, 12 * own.size),
    )(own, *parts)


def final_kernel(allow, *refs):
    got, out = refs[:-1], refs[-1]
    width = out.shape[1] // 4
    pairs = out.shape[0] // 8
    for x in range(4):
        start = 0
        for ref in got:
            number = ref.shape[0] // (16 * pairs)
            total = 0.0
            size = pairs * number
            for d2 in range(4):
                value = ref[(4 * x + d2) * size:(4 * x + d2 + 1) * size].astype(jnp.float32)
                scale = jnp.exp2(value[:, width:] * (1.0 / FINE)) * (1.0 / TOP)
                total += value[:, :width] * jnp.concatenate([scale] * (width // 128), axis=1)
            at = slice(x * width, (x + 1) * width)
            keep = allow[start:start + number, at] > 0.5
            for pair in range(pairs):
                part = total[pair * number:(pair + 1) * number]
                out[pair * 8 + start:pair * 8 + start + number, at] = jnp.where(keep, part, 0.0)
            start += number


def final(got, allow, pairs):
    width = got[0].shape[1] - 128
    last = pltpu.with_memory_space_constraint(got[-1], pltpu.VMEM)
    return pl.pallas_call(
        final_kernel,
        in_specs=[VMEM] * (1 + len(got)),
        out_specs=VMEM,
        out_shape=jax.ShapeDtypeStruct((8 * pairs, 4 * width), jnp.float32),
        compiler_params=params(24),
        cost_estimate=cost(10**7, 4 * 10**6),
    )(allow, *got[:-1], last)


def allowed(vir_counts, a_orbitals, dmax):
    labels = jnp.arange(8, dtype=jnp.int32)
    ends = jnp.sum(jnp.where(labels[:, None] <= labels[None, :], vir_counts[:, None], 0), axis=0)
    irrep = jnp.sum((a_orbitals[:, None] >= ends[None, :]).astype(jnp.int32), axis=1)
    block = jnp.bitwise_xor(labels[:, None], irrep[None, :])
    limit = jnp.sum(jnp.where(block[:, :, None] == labels, vir_counts, 0), axis=2)
    keep = jnp.arange(dmax, dtype=jnp.int32)[None, None, :] < limit[:, :, None]
    return keep.astype(jnp.float32).reshape(8, -1)


def shards(amplitudes, integrals, vir_counts, c_orbitals, a_orbitals):
    m, irreps, c_tot, dmax = amplitudes.shape
    depth = c_tot // 16 * dmax
    other = send(integrals, SWAP)
    core = lax.axis_index("pair") % 2
    by_s = jnp.swapaxes(amplitudes, 2, 3)
    starts = [sum(SPLIT[:i]) for i in range(len(SPLIT))]
    pieces = [arrange(by_s, vir_counts, c_orbitals, s, n) for s, n in zip(starts, SPLIT)]

    relaid = []
    for chunk, number in enumerate(SPLIT):
        size = 16 * m * number
        r = jnp.arange(size, dtype=jnp.int32)
        minor, d2, d1, label = r % m, r // m % 4, r // (4 * m) % 4, r // (16 * m)
        dy = jnp.where(core == 0, d1, d2)
        dz = jnp.where(core == 0, d2, d1)
        source = ((dz * 4 + dy) * m + minor) * number + label
        chooser = (source[:, None] == r[None, :]).astype(jnp.bfloat16)
        piece = pieces[chunk].reshape(16, m * number, depth)
        got = lax.all_to_all(piece, "slab", split_axis=0, concat_axis=0, tiled=True).reshape(size, depth)
        if chunk == 0:
            got, *pieces[1:] = lax.optimization_barrier((got, *pieces[1:]))
        cut = 16 * m * (number // 2)
        relaid.append([pick(part, got).astype(jnp.bfloat16) for part in (chooser[:cut], chooser[cut:])])

    products, before = [], None
    for chunk, (low, high) in enumerate(relaid):
        if before is not None:
            low, high, other, *_ = lax.optimization_barrier((low, high, other, *before))
        low1, high3 = send(low, X_DOWN), send(high, X_UP)
        high1, low3 = send(high, X_DOWN), send(low, X_UP)
        before = (high1, low3)
        if products:
            low1, high3, _ = lax.optimization_barrier((low1, high3, products[-1][0]))
        low2, high2 = send(low1, X_DOWN), send(high3, X_UP)
        arrays = [low, low1, low2, low3, high, high1, high2, high3]
        operands = (integrals, other, vir_counts, c_orbitals)
        ready = load(*operands, starts[chunk], products[-1][1] if chunk else relaid[-1][0])
        products.append(matmul(arrays[:4], arrays[4:], *operands, m, starts[chunk], ready, chunk > 0))

    sent = [[send(product[k], first(k)) for k in (1, 3, 2)] for product in products]
    results = []
    for chunk, number in enumerate(SPLIT):
        own, parts = products[chunk][0], sent[chunk]
        if chunk + 1 < len(SPLIT):
            own, *parts = lax.optimization_barrier((own, *parts, products[chunk + 1][0]))[:4]
        coded = sum_coded(own, parts, number)
        coded = coded.reshape(16, m * number, coded.shape[1])
        got = lax.all_to_all(coded, AXES, split_axis=0, concat_axis=0, tiled=True, axis_index_groups=GROUPS)
        results.append(got.reshape(16 * m * number, got.shape[2]))
    full = final(results, allowed(vir_counts, a_orbitals, dmax), m)
    return full.reshape(m, irreps, full.shape[1])


def solution(mesh):
    in_specs = (P(("pair", "slab"), None, None, None), P("slab", None, None, "pair"), P(), P(), P())
    out_specs = P(("pair", "slab"), None, None)
    return jax.shard_map(shards, mesh=mesh, in_specs=in_specs, out_specs=out_specs, check_vma=False)
```

```python
import functools

import jax
import jax.numpy as jnp
from jax import lax
from jax.experimental import pallas as pl
from jax.experimental.pallas import tpu as pltpu
from jax.sharding import PartitionSpec as P

SPLIT = (4, 4)
TOP = 32700.0
FINE = 256.0
AXES = ("slab", "pair")
MIB = 2**20
LIMIT = 52
HBM = pl.BlockSpec(memory_space=pl.ANY)
VMEM = pl.BlockSpec(memory_space=pltpu.VMEM)
SMEM = pl.BlockSpec(memory_space=pltpu.SMEM)


def place(z, y, x, core):
    return ((z % 4) * 4 + y % 4) * 8 + (x % 4) * 2 + core


def moves(target):
    return [
        (place(z, y, x, core), place(*target(z, y, x, core)))
        for z in range(4) for y in range(4) for x in range(4) for core in range(2)
    ]


X_UP = moves(lambda z, y, x, core: (z, y, x + 1, core))
X_DOWN = moves(lambda z, y, x, core: (z, y, x - 1, core))
SWAP = moves(lambda z, y, x, core: (z, y, x, 1 - core))
GROUPS = [[place(z, y, x, 0) for x in range(4) for z in range(4)] for y in range(4)]
GROUPS += [[place(z, y, x, 1) for x in range(4) for y in range(4)] for z in range(4)]


def first(k):
    return moves(lambda z, y, x, core: (z, y + k, x, core) if core == 0 else (z + k, y, x, core))


def send(value, pairs):
    return lax.ppermute(value, AXES, pairs)


def in_vmem(values):
    return [pltpu.with_memory_space_constraint(v, pltpu.VMEM) for v in values]


def cost(flops, size):
    return pl.CostEstimate(flops=flops, bytes_accessed=size, transcendentals=0)


def params(size):
    return pltpu.CompilerParams(vmem_limit_bytes=size * MIB)


def one_hot(rows, source):
    r = lax.broadcasted_iota(jnp.int32, (rows, rows), 0)
    col = lax.broadcasted_iota(jnp.int32, (rows, rows), 1)
    return (source(r) == col).astype(jnp.float32).astype(jnp.bfloat16)


def pick(matrix, value):
    return jnp.dot(matrix, value, preferred_element_type=jnp.float32)


def code_of(part):
    peak = jnp.maximum(jnp.max(jnp.abs(part), axis=1, keepdims=True), 2.0**-110)
    code = jnp.ceil(jnp.log2(peak) * FINE)
    return code, jnp.round(part * (jnp.exp2(code * (-1.0 / FINE)) * TOP))


def ends_of(counts):
    ends, total = [], 0
    for g in range(8):
        total = total + counts[g]
        ends.append(total)
    return ends


def arrange_kernel(start, count, counts, c_ref, t_ref, out, sorted_ref):
    pairs, _, dmax, c_tot = t_ref.shape
    n_slab = c_tot // 8
    rows = pairs * count
    ends = ends_of(counts)
    orbital = c_ref[...]
    irrep = sum((orbital >= ends[g]).astype(jnp.int32) for g in range(8))
    slot = lax.broadcasted_iota(jnp.int32, (dmax, c_tot), 0)
    by_c = one_hot(c_tot, lambda r: lax.rem(r, n_slab) * 8 + lax.div(r, n_slab))
    for p in range(count):
        block = jnp.bitwise_xor(irrep, start + p)
        limit = sum(jnp.where(block == g, counts[g], 0) for g in range(8))
        keep = slot < limit
        for pair in range(pairs):
            kept = jnp.where(keep, t_ref[pair, p].astype(jnp.float32), 0.0).astype(jnp.bfloat16)
            split = lax.dot_general(by_c, kept, (((1,), (1,)), ((), ())), preferred_element_type=jnp.float32)
            split = split.astype(jnp.bfloat16)
            q = pair * count + p
            for c in range(8):
                sorted_ref[c, q * n_slab:(q + 1) * n_slab] = split[c * n_slab:(c + 1) * n_slab]
    by_slab = one_hot(n_slab * rows, lambda r: lax.rem(r, rows) * n_slab + lax.div(r, rows))
    for i in range(4):
        both = [pick(by_slab, sorted_ref[2 * i + h]) for h in range(2)]
        out[:, i * 2 * dmax:(i + 1) * 2 * dmax] = jnp.concatenate(both, axis=1).astype(jnp.bfloat16)


def arrange(amplitudes, vir_counts, c_orbitals, start, count):
    rows, _, dmax, c_tot = amplitudes.shape
    size = c_tot // 8 * rows * count
    return pl.pallas_call(
        functools.partial(arrange_kernel, start, count),
        grid=(1,),
        in_specs=[
            SMEM,
            pl.BlockSpec((1, c_tot), lambda i: (0, 0)),
            pl.BlockSpec((rows, count, dmax, c_tot), lambda i: (0, start // count, 0, 0)),
        ],
        out_specs=pl.BlockSpec((size, 8 * dmax), lambda i: (0, 0)),
        out_shape=jax.ShapeDtypeStruct((size, 8 * dmax), jnp.bfloat16),
        scratch_shapes=[pltpu.VMEM((8, size, dmax), jnp.bfloat16)],
        compiler_params=params(58),
        cost_estimate=cost(2 * 10**9, 4 * 10**6),
    )(vir_counts, c_orbitals.reshape(1, c_tot), amplitudes)


def copies_of(sides, counts, c_orbitals, label, target, sems):
    c_dev, _, dmax, _ = sides[0].shape
    ends = ends_of(counts)
    slab = lax.axis_index("slab")
    copies = []
    for c in range(c_dev):
        orbital = c_orbitals[slab * c_dev + c]
        irrep = sum((orbital >= ends[g]).astype(jnp.int32) for g in range(8))
        for side, ref in enumerate(sides):
            copies.append(pltpu.make_async_copy(
                ref.at[c, jnp.bitwise_xor(irrep, label)], target.at[side, pl.ds(c * dmax, dmax)], sems.at[side, c]
            ))
    return copies


def load_kernel(label, counts, c_orbitals, v_own, v_other, after, out, sems):
    del after
    copies = copies_of((v_own, v_other), counts, c_orbitals, label, out, sems)
    for copy in copies:
        copy.start()
    for copy in copies:
        copy.wait()


def load(v_own, v_other, vir_counts, c_orbitals, label, after):
    c_dev, _, dmax, half = v_own.shape
    return pl.pallas_call(
        functools.partial(load_kernel, label),
        in_specs=[SMEM, SMEM, HBM, HBM, HBM],
        out_specs=VMEM,
        out_shape=pltpu.VMEM((2, c_dev * dmax, half), jnp.bfloat16),
        scratch_shapes=[pltpu.SemaphoreType.DMA((2, c_dev))],
        compiler_params=params(LIMIT),
        cost_estimate=cost(0, v_own.size),
    )(vir_counts, c_orbitals, v_own, v_other, after)


def matmul_kernel(m, start, counts, c_orbitals, *refs):
    lows, highs, sides = refs[:4], refs[4:8], refs[8:10]
    ready = refs[10]
    outs = refs[-14:-10]
    lhs, slots, even, odd, own, coded, codes, sems, v_sems, o_sems = refs[-10:]
    number, _, rows, depth = lhs.shape
    half = sides[0].shape[3]
    width = 2 * half
    split = lows[0].shape[0]
    slab, pair = lax.axis_index("slab"), lax.axis_index("pair")
    x, core = lax.div(pair, 2), lax.rem(pair, 2)
    me = jnp.where(core == 0, lax.rem(slab, 4), lax.div(slab, 4))

    def fetch(p):
        if p == 0:
            return []
        return copies_of(sides, counts, c_orbitals, start + p, slots.at[p % 3], v_sems.at[p % 3])

    def arrivals(refs, first_p, at):
        return [
            pltpu.make_async_copy(ref, lhs.at[pl.ds(first_p, ref.shape[0]), lax.rem(x + r, 4)], sems.at[at + r])
            for r, ref in enumerate(refs)
        ]

    low, high = arrivals(lows, 0, 0), arrivals(highs, split, 4)
    for copy in low + fetch(0) + high + fetch(1):
        copy.start()
    codes[...] = jnp.zeros_like(codes)
    lane = lax.broadcasted_iota(jnp.int32, (rows, 128), 1)
    started = []

    def finish(p, ref):
        at = slice(p * width, (p + 1) * width)
        for k in range(4):
            d1 = lax.rem(me + k, 4)
            part = jnp.concatenate([ref[4 * r + d1] for r in range(4)], axis=0)
            if k == 0:
                own[:, at] = part
                source = own.at[:, at]
            else:
                code, value = code_of(part)
                coded[k - 1, :, at] = value.astype(jnp.int16)
                codes[k - 1] = jnp.where(lane == p, code, codes[k - 1])
                source = coded.at[k - 1, :, at]
            started.append(pltpu.make_async_copy(source, outs[k].at[:, at], o_sems.at[p, k]))
            started[-1].start()

    products = (even, odd)
    for p in range(number):
        if p in (0, split):
            for copy in (high if p else low):
                copy.wait()
        if p + 2 < number:
            for copy in fetch(p + 2):
                copy.start()
        for copy in fetch(p):
            copy.wait()
        left = lhs[p].reshape(4 * rows, depth)
        for side, at in ((0, core), (1, 1 - core)):
            at = pl.ds(pl.multiple_of(at * half, 128), half)
            right = slots[p % 3, side] if p else ready[side]
            products[p % 2][:, :, at] = pick(left, right).reshape(16, 4 * m, half)
        if p > 0:
            finish(p - 1, products[(p - 1) % 2])
    finish(number - 1, products[(number - 1) % 2])
    at = slice(number * width, number * width + 128)
    for k in range(1, 4):
        coded[k - 1, :, at] = codes[k - 1].astype(jnp.int16)
        started.append(pltpu.make_async_copy(coded.at[k - 1, :, at], outs[k].at[:, at], o_sems.at[number, k]))
        started[-1].start()
    for copy in started:
        copy.wait()


def matmul(lows, highs, v_own, v_other, vir_counts, c_orbitals, m, start, ready, near):
    c_dev, _, dmax, half = v_own.shape
    rows, depth, width = 16 * m, c_dev * dmax, 2 * half
    arrays = [a.reshape(-1, rows, depth) for a in lows + highs]
    number = arrays[0].shape[0] + arrays[-1].shape[0]
    shapes = [jax.ShapeDtypeStruct((rows, number * width), jnp.float32)]
    shapes += [jax.ShapeDtypeStruct((rows, number * width + 128), jnp.int16)] * 3
    if near:
        arrays = in_vmem(arrays)
    return pl.pallas_call(
        functools.partial(matmul_kernel, m, start),
        in_specs=[SMEM] * 2 + [VMEM if near else HBM] * 8 + [HBM] * 2 + [VMEM],
        out_specs=[HBM] * 4,
        out_shape=shapes,
        scratch_shapes=[
            pltpu.VMEM((number, 4, rows, depth), jnp.bfloat16),
            pltpu.VMEM((3, 2, depth, half), jnp.bfloat16),
            pltpu.VMEM((16, 4 * m, width), jnp.float32),
            pltpu.VMEM((16, 4 * m, width), jnp.float32),
            pltpu.VMEM((rows, number * width), jnp.float32),
            pltpu.VMEM((3, rows, number * width + 128), jnp.int16),
            pltpu.VMEM((3, rows, 128), jnp.float32),
            pltpu.SemaphoreType.DMA((8,)),
            pltpu.SemaphoreType.DMA((3, 2, 8)),
            pltpu.SemaphoreType.DMA((number + 1, 4)),
        ],
        compiler_params=params(LIMIT),
        cost_estimate=cost(2 * number * 4 * rows * depth * width, number * v_own.size // 2),
    )(vir_counts, c_orbitals, *arrays, v_own, v_other, *in_vmem([ready]))


def sum_kernel(number, own_ref, q1, q2, q3, out, own, q, mixed, sems):
    rows = own.shape[0]
    width = own.shape[1] // number
    tail = slice(number * width, number * width + 128)
    codes = [pltpu.make_async_copy(ref.at[:, tail], q.at[k, :, tail], sems.at[number, k]) for k, ref in enumerate((q1, q2, q3))]
    copies = []
    for p in range(number):
        at = slice(p * width, (p + 1) * width)
        copies.append([pltpu.make_async_copy(own_ref.at[:, at], own.at[:, at], sems.at[p, 3])])
        for k, ref in enumerate((q1, q2, q3)):
            copies[p].append(pltpu.make_async_copy(ref.at[:, at], q.at[k, :, at], sems.at[p, k]))
    for group in [codes] + copies:
        for copy in group:
            copy.start()
    lane = lax.broadcasted_iota(jnp.int32, (rows, 128), 1)
    for copy in codes:
        copy.wait()
    scales = [jnp.exp2(q[k, :, tail].astype(jnp.float32) * (1.0 / FINE)) * (1.0 / TOP) for k in range(3)]
    for p in range(number):
        for copy in copies[p]:
            copy.wait()
        at = slice(p * width, (p + 1) * width)
        total = own[:, at]
        for k in range(3):
            one = jnp.sum(jnp.where(lane == p, scales[k], 0.0), axis=1, keepdims=True)
            total += q[k, :, at].astype(jnp.float32) * one
        code, value = code_of(total)
        value = jnp.concatenate([value, jnp.broadcast_to(code, (rows, 128))], axis=1)
        for j in range(mixed.shape[0]):
            mixed[j, pl.ds(p, rows, number), :] = value[:, j * 128:(j + 1) * 128]
    for j in range(mixed.shape[0]):
        out[:, j * 128:(j + 1) * 128] = mixed[j].astype(jnp.int16)


def sum_coded(own, parts, number):
    rows, total = own.shape
    width = total // number + 128
    return pl.pallas_call(
        functools.partial(sum_kernel, number),
        in_specs=[HBM] * 4,
        out_specs=VMEM,
        out_shape=jax.ShapeDtypeStruct((number * rows, width), jnp.int16),
        scratch_shapes=[
            pltpu.VMEM(own.shape, jnp.float32),
            pltpu.VMEM((3,) + parts[0].shape, jnp.int16),
            pltpu.VMEM((width // 128, number * rows, 128), jnp.float32),
            pltpu.SemaphoreType.DMA((number + 1, 4)),
        ],
        compiler_params=params(LIMIT),
        cost_estimate=cost(8 * own.size, 12 * own.size),
    )(own, *in_vmem(parts))


def final_kernel(allow, *refs):
    got, out = refs[:-1], refs[-1]
    width = out.shape[1] // 4
    pairs = out.shape[0] // 8
    for x in range(4):
        start = 0
        for ref in got:
            number = ref.shape[0] // (16 * pairs)
            total = 0.0
            size = pairs * number
            for d2 in range(4):
                value = ref[(4 * x + d2) * size:(4 * x + d2 + 1) * size].astype(jnp.float32)
                scale = jnp.exp2(value[:, width:] * (1.0 / FINE)) * (1.0 / TOP)
                total += value[:, :width] * jnp.concatenate([scale] * (width // 128), axis=1)
            at = slice(x * width, (x + 1) * width)
            keep = allow[start:start + number, at] > 0.5
            for pair in range(pairs):
                part = total[pair * number:(pair + 1) * number]
                out[pair * 8 + start:pair * 8 + start + number, at] = jnp.where(keep, part, 0.0)
            start += number


def final(got, allow, pairs):
    width = got[0].shape[1] - 128
    last = pltpu.with_memory_space_constraint(got[-1], pltpu.VMEM)
    return pl.pallas_call(
        final_kernel,
        in_specs=[VMEM] * (1 + len(got)),
        out_specs=VMEM,
        out_shape=jax.ShapeDtypeStruct((8 * pairs, 4 * width), jnp.float32),
        compiler_params=params(24),
        cost_estimate=cost(10**7, 4 * 10**6),
    )(allow, *got[:-1], last)


def allowed(vir_counts, a_orbitals, dmax):
    labels = jnp.arange(8, dtype=jnp.int32)
    ends = jnp.sum(jnp.where(labels[:, None] <= labels[None, :], vir_counts[:, None], 0), axis=0)
    irrep = jnp.sum((a_orbitals[:, None] >= ends[None, :]).astype(jnp.int32), axis=1)
    block = jnp.bitwise_xor(labels[:, None], irrep[None, :])
    limit = jnp.sum(jnp.where(block[:, :, None] == labels, vir_counts, 0), axis=2)
    keep = jnp.arange(dmax, dtype=jnp.int32)[None, None, :] < limit[:, :, None]
    return keep.astype(jnp.float32).reshape(8, -1)


def shards(amplitudes, integrals, vir_counts, c_orbitals, a_orbitals):
    m, irreps, c_tot, dmax = amplitudes.shape
    depth = c_tot // 16 * dmax
    other = send(integrals, SWAP)
    core = lax.axis_index("pair") % 2
    by_s = jnp.swapaxes(amplitudes, 2, 3)
    starts = [sum(SPLIT[:i]) for i in range(len(SPLIT))]
    pieces = [arrange(by_s, vir_counts, c_orbitals, s, n) for s, n in zip(starts, SPLIT)]

    relaid = []
    for chunk, number in enumerate(SPLIT):
        size = 16 * m * number
        r = jnp.arange(size, dtype=jnp.int32)
        minor, d2, d1, label = r % m, r // m % 4, r // (4 * m) % 4, r // (16 * m)
        dy = jnp.where(core == 0, d1, d2)
        dz = jnp.where(core == 0, d2, d1)
        source = ((dz * 4 + dy) * m + minor) * number + label
        chooser = (source[:, None] == r[None, :]).astype(jnp.bfloat16)
        piece = pieces[chunk].reshape(16, m * number, depth)
        got = lax.all_to_all(piece, "slab", split_axis=0, concat_axis=0, tiled=True).reshape(size, depth)
        if chunk == 0:
            got, *pieces[1:] = lax.optimization_barrier((got, *pieces[1:]))
        cut = 16 * m * (number // 2)
        relaid.append([pick(part, got).astype(jnp.bfloat16) for part in (chooser[:cut], chooser[cut:])])

    products, before = [], None
    for chunk, (low, high) in enumerate(relaid):
        if before is not None:
            low, high, other, *_ = lax.optimization_barrier((low, high, other, *before))
        low1, high3 = send(low, X_DOWN), send(high, X_UP)
        high1, low3 = send(high, X_DOWN), send(low, X_UP)
        before = (high1, low3)
        if products:
            low1, high3, _ = lax.optimization_barrier((low1, high3, products[-1][0]))
        low2, high2 = send(low1, X_DOWN), send(high3, X_UP)
        arrays = [low, low1, low2, low3, high, high1, high2, high3]
        operands = (integrals, other, vir_counts, c_orbitals)
        ready = load(*operands, starts[chunk], products[-1][1] if chunk else relaid[-1][0])
        products.append(matmul(arrays[:4], arrays[4:], *operands, m, starts[chunk], ready, chunk > 0))

    sent = [[send(product[k], first(k)) for k in (1, 3, 2)] for product in products]
    results = []
    for chunk, number in enumerate(SPLIT):
        own, parts = products[chunk][0], sent[chunk]
        if chunk + 1 < len(SPLIT):
            own, *parts = lax.optimization_barrier((own, *parts, products[chunk + 1][0]))[:4]
        coded = sum_coded(own, parts, number)
        coded = coded.reshape(16, m * number, coded.shape[1])
        got = lax.all_to_all(coded, AXES, split_axis=0, concat_axis=0, tiled=True, axis_index_groups=GROUPS)
        results.append(got.reshape(16 * m * number, got.shape[2]))
    full = final(results, allowed(vir_counts, a_orbitals, dmax), m)
    return full.reshape(m, irreps, full.shape[1])


def solution(mesh):
    in_specs = (P(("pair", "slab"), None, None, None), P("slab", None, None, "pair"), P(), P(), P())
    out_specs = P(("pair", "slab"), None, None)
    return jax.shard_map(shards, mesh=mesh, in_specs=in_specs, out_specs=out_specs, check_vma=False)
```

```python
import functools

import jax
import jax.numpy as jnp
from jax import lax
from jax.experimental import pallas as pl
from jax.experimental.pallas import tpu as pltpu
from jax.sharding import PartitionSpec as P

SPLIT = (4, 4)
TOP = 32700.0
FINE = 256.0
AXES = ("slab", "pair")
MIB = 2**20
LIMIT = 52
HBM = pl.BlockSpec(memory_space=pl.ANY)
VMEM = pl.BlockSpec(memory_space=pltpu.VMEM)
SMEM = pl.BlockSpec(memory_space=pltpu.SMEM)


def place(z, y, x, core):
    return ((z % 4) * 4 + y % 4) * 8 + (x % 4) * 2 + core


def moves(target):
    return [
        (place(z, y, x, core), place(*target(z, y, x, core)))
        for z in range(4) for y in range(4) for x in range(4) for core in range(2)
    ]


X_UP = moves(lambda z, y, x, core: (z, y, x + 1, core))
X_DOWN = moves(lambda z, y, x, core: (z, y, x - 1, core))
SWAP = moves(lambda z, y, x, core: (z, y, x, 1 - core))
GROUPS = [[place(z, y, x, 0) for x in range(4) for z in range(4)] for y in range(4)]
GROUPS += [[place(z, y, x, 1) for x in range(4) for y in range(4)] for z in range(4)]


def first(k):
    return moves(lambda z, y, x, core: (z, y + k, x, core) if core == 0 else (z + k, y, x, core))


def send(value, pairs):
    return lax.ppermute(value, AXES, pairs)


def in_vmem(values):
    return [pltpu.with_memory_space_constraint(v, pltpu.VMEM) for v in values]


def cost(flops, size):
    return pl.CostEstimate(flops=flops, bytes_accessed=size, transcendentals=0)


def params(size):
    return pltpu.CompilerParams(vmem_limit_bytes=size * MIB)


def one_hot(rows, source):
    r = lax.broadcasted_iota(jnp.int32, (rows, rows), 0)
    col = lax.broadcasted_iota(jnp.int32, (rows, rows), 1)
    return (source(r) == col).astype(jnp.float32).astype(jnp.bfloat16)


def pick(matrix, value):
    return jnp.dot(matrix, value, preferred_element_type=jnp.float32)


def code_of(part):
    peak = jnp.maximum(jnp.max(jnp.abs(part), axis=1, keepdims=True), 2.0**-110)
    code = jnp.ceil(jnp.log2(peak) * FINE)
    return code, jnp.round(part * (jnp.exp2(code * (-1.0 / FINE)) * TOP))


def ends_of(counts):
    ends, total = [], 0
    for g in range(8):
        total = total + counts[g]
        ends.append(total)
    return ends


def arrange_kernel(start, count, counts, c_ref, t_ref, out, sorted_ref):
    pairs, _, dmax, c_tot = t_ref.shape
    n_slab = c_tot // 8
    rows = pairs * count
    ends = ends_of(counts)
    orbital = c_ref[...]
    irrep = sum((orbital >= ends[g]).astype(jnp.int32) for g in range(8))
    slot = lax.broadcasted_iota(jnp.int32, (dmax, c_tot), 0)
    by_c = one_hot(c_tot, lambda r: lax.rem(r, n_slab) * 8 + lax.div(r, n_slab))
    for p in range(count):
        block = jnp.bitwise_xor(irrep, start + p)
        limit = sum(jnp.where(block == g, counts[g], 0) for g in range(8))
        keep = slot < limit
        for pair in range(pairs):
            kept = jnp.where(keep, t_ref[pair, p].astype(jnp.float32), 0.0).astype(jnp.bfloat16)
            split = lax.dot_general(by_c, kept, (((1,), (1,)), ((), ())), preferred_element_type=jnp.float32)
            split = split.astype(jnp.bfloat16)
            q = pair * count + p
            for c in range(8):
                sorted_ref[c, q * n_slab:(q + 1) * n_slab] = split[c * n_slab:(c + 1) * n_slab]
    by_slab = one_hot(n_slab * rows, lambda r: lax.rem(r, rows) * n_slab + lax.div(r, rows))
    for i in range(4):
        both = [pick(by_slab, sorted_ref[2 * i + h]) for h in range(2)]
        out[:, i * 2 * dmax:(i + 1) * 2 * dmax] = jnp.concatenate(both, axis=1).astype(jnp.bfloat16)


def arrange(amplitudes, vir_counts, c_orbitals, start, count):
    rows, _, dmax, c_tot = amplitudes.shape
    size = c_tot // 8 * rows * count
    return pl.pallas_call(
        functools.partial(arrange_kernel, start, count),
        grid=(1,),
        in_specs=[
            SMEM,
            pl.BlockSpec((1, c_tot), lambda i: (0, 0)),
            pl.BlockSpec((rows, count, dmax, c_tot), lambda i: (0, start // count, 0, 0)),
        ],
        out_specs=pl.BlockSpec((size, 8 * dmax), lambda i: (0, 0)),
        out_shape=jax.ShapeDtypeStruct((size, 8 * dmax), jnp.bfloat16),
        scratch_shapes=[pltpu.VMEM((8, size, dmax), jnp.bfloat16)],
        compiler_params=params(58),
        cost_estimate=cost(2 * 10**9, 4 * 10**6),
    )(vir_counts, c_orbitals.reshape(1, c_tot), amplitudes)


def copies_of(sides, counts, c_orbitals, label, target, sems):
    c_dev, _, dmax, _ = sides[0].shape
    ends = ends_of(counts)
    slab = lax.axis_index("slab")
    copies = []
    for c in range(c_dev):
        orbital = c_orbitals[slab * c_dev + c]
        irrep = sum((orbital >= ends[g]).astype(jnp.int32) for g in range(8))
        for side, ref in enumerate(sides):
            copies.append(pltpu.make_async_copy(
                ref.at[c, jnp.bitwise_xor(irrep, label)], target.at[side, pl.ds(c * dmax, dmax)], sems.at[side, c]
            ))
    return copies


def load_kernel(label, counts, c_orbitals, v_own, v_other, after, out, sems):
    del after
    copies = copies_of((v_own, v_other), counts, c_orbitals, label, out, sems)
    for copy in copies:
        copy.start()
    for copy in copies:
        copy.wait()


def load(v_own, v_other, vir_counts, c_orbitals, label, after):
    c_dev, _, dmax, half = v_own.shape
    return pl.pallas_call(
        functools.partial(load_kernel, label),
        in_specs=[SMEM, SMEM, HBM, HBM, HBM],
        out_specs=VMEM,
        out_shape=pltpu.VMEM((2, c_dev * dmax, half), jnp.bfloat16),
        scratch_shapes=[pltpu.SemaphoreType.DMA((2, c_dev))],
        compiler_params=params(LIMIT),
        cost_estimate=cost(0, v_own.size),
    )(vir_counts, c_orbitals, v_own, v_other, after)


def matmul_kernel(m, start, counts, c_orbitals, *refs):
    lows, highs, sides = refs[:4], refs[4:8], refs[8:10]
    ready = refs[10]
    outs = refs[-14:-10]
    lhs, slots, even, odd, own, coded, codes, sems, v_sems, o_sems = refs[-10:]
    number, _, rows, depth = lhs.shape
    half = sides[0].shape[3]
    width = 2 * half
    split = lows[0].shape[0]
    slab, pair = lax.axis_index("slab"), lax.axis_index("pair")
    x, core = lax.div(pair, 2), lax.rem(pair, 2)
    me = jnp.where(core == 0, lax.rem(slab, 4), lax.div(slab, 4))

    def fetch(p):
        if p == 0:
            return []
        return copies_of(sides, counts, c_orbitals, start + p, slots.at[p % 3], v_sems.at[p % 3])

    def arrivals(refs, first_p, at):
        return [
            pltpu.make_async_copy(ref, lhs.at[pl.ds(first_p, ref.shape[0]), lax.rem(x + r, 4)], sems.at[at + r])
            for r, ref in enumerate(refs)
        ]

    low, high = arrivals(lows, 0, 0), arrivals(highs, split, 4)
    for copy in low + fetch(0) + high + fetch(1):
        copy.start()
    codes[...] = jnp.zeros_like(codes)
    lane = lax.broadcasted_iota(jnp.int32, (rows, 128), 1)
    started = []

    def finish(p, ref):
        at = slice(p * width, (p + 1) * width)
        for k in range(4):
            d1 = lax.rem(me + k, 4)
            part = jnp.concatenate([ref[4 * r + d1] for r in range(4)], axis=0)
            if k == 0:
                own[:, at] = part
                source = own.at[:, at]
            else:
                code, value = code_of(part)
                coded[k - 1, :, at] = value.astype(jnp.int16)
                codes[k - 1] = jnp.where(lane == p, code, codes[k - 1])
                source = coded.at[k - 1, :, at]
            started.append(pltpu.make_async_copy(source, outs[k].at[:, at], o_sems.at[p, k]))
            started[-1].start()

    products = (even, odd)
    for p in range(number):
        if p in (0, split):
            for copy in (high if p else low):
                copy.wait()
        if p + 2 < number:
            for copy in fetch(p + 2):
                copy.start()
        for copy in fetch(p):
            copy.wait()
        left = lhs[p].reshape(4 * rows, depth)
        for side, at in ((0, core), (1, 1 - core)):
            at = pl.ds(pl.multiple_of(at * half, 128), half)
            right = slots[p % 3, side] if p else ready[side]
            products[p % 2][:, :, at] = pick(left, right).reshape(16, 4 * m, half)
        if p > 0:
            finish(p - 1, products[(p - 1) % 2])
    finish(number - 1, products[(number - 1) % 2])
    at = slice(number * width, number * width + 128)
    for k in range(1, 4):
        coded[k - 1, :, at] = codes[k - 1].astype(jnp.int16)
        started.append(pltpu.make_async_copy(coded.at[k - 1, :, at], outs[k].at[:, at], o_sems.at[number, k]))
        started[-1].start()
    for copy in started:
        copy.wait()


def matmul(lows, highs, v_own, v_other, vir_counts, c_orbitals, m, start, ready, near):
    c_dev, _, dmax, half = v_own.shape
    rows, depth, width = 16 * m, c_dev * dmax, 2 * half
    arrays = [a.reshape(-1, rows, depth) for a in lows + highs]
    number = arrays[0].shape[0] + arrays[-1].shape[0]
    shapes = [jax.ShapeDtypeStruct((rows, number * width), jnp.float32)]
    shapes += [jax.ShapeDtypeStruct((rows, number * width + 128), jnp.int16)] * 3
    if near:
        arrays = in_vmem(arrays)
    return pl.pallas_call(
        functools.partial(matmul_kernel, m, start),
        in_specs=[SMEM] * 2 + [VMEM if near else HBM] * 8 + [HBM] * 2 + [VMEM],
        out_specs=[HBM] * 4,
        out_shape=shapes,
        scratch_shapes=[
            pltpu.VMEM((number, 4, rows, depth), jnp.bfloat16),
            pltpu.VMEM((3, 2, depth, half), jnp.bfloat16),
            pltpu.VMEM((16, 4 * m, width), jnp.float32),
            pltpu.VMEM((16, 4 * m, width), jnp.float32),
            pltpu.VMEM((rows, number * width), jnp.float32),
            pltpu.VMEM((3, rows, number * width + 128), jnp.int16),
            pltpu.VMEM((3, rows, 128), jnp.float32),
            pltpu.SemaphoreType.DMA((8,)),
            pltpu.SemaphoreType.DMA((3, 2, 8)),
            pltpu.SemaphoreType.DMA((number + 1, 4)),
        ],
        compiler_params=params(LIMIT),
        cost_estimate=cost(2 * number * 4 * rows * depth * width, number * v_own.size // 2),
    )(vir_counts, c_orbitals, *arrays, v_own, v_other, *in_vmem([ready]))


def sum_kernel(number, own_ref, q1, q2, q3, out, own, q, mixed, sems):
    rows = own.shape[0]
    width = own.shape[1] // number
    tail = slice(number * width, number * width + 128)
    codes = [pltpu.make_async_copy(ref.at[:, tail], q.at[k, :, tail], sems.at[number, k]) for k, ref in enumerate((q1, q2, q3))]
    copies = []
    for p in range(number):
        at = slice(p * width, (p + 1) * width)
        copies.append([pltpu.make_async_copy(own_ref.at[:, at], own.at[:, at], sems.at[p, 3])])
        for k, ref in enumerate((q1, q2, q3)):
            copies[p].append(pltpu.make_async_copy(ref.at[:, at], q.at[k, :, at], sems.at[p, k]))
    for group in [codes] + copies:
        for copy in group:
            copy.start()
    lane = lax.broadcasted_iota(jnp.int32, (rows, 128), 1)
    for copy in codes:
        copy.wait()
    scales = [jnp.exp2(q[k, :, tail].astype(jnp.float32) * (1.0 / FINE)) * (1.0 / TOP) for k in range(3)]
    for p in range(number):
        for copy in copies[p]:
            copy.wait()
        at = slice(p * width, (p + 1) * width)
        total = own[:, at]
        for k in range(3):
            one = jnp.sum(jnp.where(lane == p, scales[k], 0.0), axis=1, keepdims=True)
            total += q[k, :, at].astype(jnp.float32) * one
        code, value = code_of(total)
        value = jnp.concatenate([value, jnp.broadcast_to(code, (rows, 128))], axis=1)
        for j in range(mixed.shape[0]):
            mixed[j, pl.ds(p, rows, number), :] = value[:, j * 128:(j + 1) * 128]
    for j in range(mixed.shape[0]):
        out[:, j * 128:(j + 1) * 128] = mixed[j].astype(jnp.int16)


def sum_coded(own, parts, number):
    rows, total = own.shape
    width = total // number + 128
    return pl.pallas_call(
        functools.partial(sum_kernel, number),
        in_specs=[HBM] * 4,
        out_specs=VMEM,
        out_shape=pltpu.VMEM((number * rows, width), jnp.int16),
        scratch_shapes=[
            pltpu.VMEM(own.shape, jnp.float32),
            pltpu.VMEM((3,) + parts[0].shape, jnp.int16),
            pltpu.VMEM((width // 128, number * rows, 128), jnp.float32),
            pltpu.SemaphoreType.DMA((number + 1, 4)),
        ],
        compiler_params=params(LIMIT),
        cost_estimate=cost(8 * own.size, 12 * own.size),
    )(own, *in_vmem(parts))


def final_kernel(allow, *refs):
    got, out = refs[:-1], refs[-1]
    width = out.shape[1] // 4
    pairs = out.shape[0] // 8
    for x in range(4):
        start = 0
        for ref in got:
            number = ref.shape[0] // (16 * pairs)
            total = 0.0
            size = pairs * number
            for d2 in range(4):
                value = ref[(4 * x + d2) * size:(4 * x + d2 + 1) * size].astype(jnp.float32)
                scale = jnp.exp2(value[:, width:] * (1.0 / FINE)) * (1.0 / TOP)
                total += value[:, :width] * jnp.concatenate([scale] * (width // 128), axis=1)
            at = slice(x * width, (x + 1) * width)
            keep = allow[start:start + number, at] > 0.5
            for pair in range(pairs):
                part = total[pair * number:(pair + 1) * number]
                out[pair * 8 + start:pair * 8 + start + number, at] = jnp.where(keep, part, 0.0)
            start += number


def final(got, allow, pairs):
    width = got[0].shape[1] - 128
    last = pltpu.with_memory_space_constraint(got[-1], pltpu.VMEM)
    return pl.pallas_call(
        final_kernel,
        in_specs=[VMEM] * (1 + len(got)),
        out_specs=VMEM,
        out_shape=jax.ShapeDtypeStruct((8 * pairs, 4 * width), jnp.float32),
        compiler_params=params(24),
        cost_estimate=cost(10**7, 4 * 10**6),
    )(allow, *got[:-1], last)


def allowed(vir_counts, a_orbitals, dmax):
    labels = jnp.arange(8, dtype=jnp.int32)
    ends = jnp.sum(jnp.where(labels[:, None] <= labels[None, :], vir_counts[:, None], 0), axis=0)
    irrep = jnp.sum((a_orbitals[:, None] >= ends[None, :]).astype(jnp.int32), axis=1)
    block = jnp.bitwise_xor(labels[:, None], irrep[None, :])
    limit = jnp.sum(jnp.where(block[:, :, None] == labels, vir_counts, 0), axis=2)
    keep = jnp.arange(dmax, dtype=jnp.int32)[None, None, :] < limit[:, :, None]
    return keep.astype(jnp.float32).reshape(8, -1)


def shards(amplitudes, integrals, vir_counts, c_orbitals, a_orbitals):
    m, irreps, c_tot, dmax = amplitudes.shape
    depth = c_tot // 16 * dmax
    other = send(integrals, SWAP)
    core = lax.axis_index("pair") % 2
    by_s = jnp.swapaxes(amplitudes, 2, 3)
    starts = [sum(SPLIT[:i]) for i in range(len(SPLIT))]
    pieces = [arrange(by_s, vir_counts, c_orbitals, s, n) for s, n in zip(starts, SPLIT)]

    relaid = []
    for chunk, number in enumerate(SPLIT):
        size = 16 * m * number
        r = jnp.arange(size, dtype=jnp.int32)
        minor, d2, d1, label = r % m, r // m % 4, r // (4 * m) % 4, r // (16 * m)
        dy = jnp.where(core == 0, d1, d2)
        dz = jnp.where(core == 0, d2, d1)
        source = ((dz * 4 + dy) * m + minor) * number + label
        chooser = (source[:, None] == r[None, :]).astype(jnp.bfloat16)
        piece = pieces[chunk].reshape(16, m * number, depth)
        got = lax.all_to_all(piece, "slab", split_axis=0, concat_axis=0, tiled=True).reshape(size, depth)
        if chunk == 0:
            got, *pieces[1:] = lax.optimization_barrier((got, *pieces[1:]))
        cut = 16 * m * (number // 2)
        relaid.append([pick(part, got).astype(jnp.bfloat16) for part in (chooser[:cut], chooser[cut:])])

    products, before = [], None
    for chunk, (low, high) in enumerate(relaid):
        if before is not None:
            low, high, other, *_ = lax.optimization_barrier((low, high, other, *before))
        low1, high3 = send(low, X_DOWN), send(high, X_UP)
        high1, low3 = send(high, X_DOWN), send(low, X_UP)
        before = (low1, high3)
        if products:
            low1, high3, _ = lax.optimization_barrier((low1, high3, products[-1][0]))
        low2, high2 = send(low1, X_DOWN), send(high3, X_UP)
        arrays = [low, low1, low2, low3, high, high1, high2, high3]
        operands = (integrals, other, vir_counts, c_orbitals)
        ready = load(*operands, starts[chunk], products[-1][1] if chunk else relaid[-1][0])
        products.append(matmul(arrays[:4], arrays[4:], *operands, m, starts[chunk], ready, chunk > 0))

    sent = [[send(product[k], first(k)) for k in (1, 3, 2)] for product in products]
    results = []
    for chunk, number in enumerate(SPLIT):
        own, parts = products[chunk][0], sent[chunk]
        if chunk + 1 < len(SPLIT):
            own, *parts = lax.optimization_barrier((own, *parts, products[chunk + 1][0]))[:4]
        coded = sum_coded(own, parts, number)
        coded = coded.reshape(16, m * number, coded.shape[1])
        got = lax.all_to_all(coded, AXES, split_axis=0, concat_axis=0, tiled=True, axis_index_groups=GROUPS)
        results.append(got.reshape(16 * m * number, got.shape[2]))
    full = final(results, allowed(vir_counts, a_orbitals, dmax), m)
    return full.reshape(m, irreps, full.shape[1])


def solution(mesh):
    in_specs = (P(("pair", "slab"), None, None, None), P("slab", None, None, "pair"), P(), P(), P())
    out_specs = P(("pair", "slab"), None, None)
    return jax.shard_map(shards, mesh=mesh, in_specs=in_specs, out_specs=out_specs, check_vma=False)
```
